512 devices in a mesh: attn: 4 (over x), grp: 4 (over z_hi), exp: 32 (over z_lo, y, core).
Axes of the slice: x: 4, y: 8, z: 8 (z_hi: 4, z_lo: 2; z = z_hi * 2 + z_lo), core: 2. Of those that a mesh axis runs over, the one named last changes fastest.
Arguments:
- resid: bfloat16 [2, 128, 3584], P(None, 'grp'), may hold values from -36 to 36
- queries: bfloat16 [2, 128, 64, 576], P(None, ('grp', 'exp')), may hold values from -49 to 49
- cache: bfloat16 [2, 128, 2048, 576], P(None, ('grp', 'exp'), 'attn'), may hold values from -4 to 4
- lengths: int32 [2, 128], P(None, ('grp', 'exp')), may hold values from 2 to 2048, as said below
- w_value: bfloat16 [64, 512, 128], P('exp', None, 'attn'), may hold values from -2 to 2
- w_out: bfloat16 [64, 128, 3584], P('exp', 'attn'), may hold values from -0.0625 to 0.0625
- norm_gain: bfloat16 [3584], replicated, may hold values from 0.099609375 to 1.8984375
- route_ids: int32 [2, 128, 8], replicated, may hold values from 0 to 31, all different within a row; in each aligned block of 32 rows (0 to 31, 32 to 63, ..., all dimensions but the last counted through in order) at most 16 rows name the same one
- route_weights: float32 [2, 128, 8], replicated, may hold values from 0.05 to 1
- w_gate: bfloat16 [32, 3584, 2048], P('exp', None, ('attn', 'grp')), may hold values from -0.09375 to 0.09375
- w_up: bfloat16 [32, 3584, 2048], P('exp', None, ('attn', 'grp')), may hold values from -0.09375 to 0.09375
- w_down: bfloat16 [32, 2048, 3584], P('exp', ('attn', 'grp')), may hold values from -0.125 to 0.125
Outputs:
- layer_out: bfloat16 [2, 128, 3584], P(None, ('grp', 'exp'), 'attn')
The draws below stay inside these ranges and needn't reach their ends.
Inputs may be any that keep to these rules, and one draw needn't show every extreme that they name: `route_ids`: each row names 8 different experts; among the 32 tokens of one group in one micro-batch (aligned blocks of rows) no expert is named more than 16 times, a bound that some block reaches. `lengths`: each micro-batch has a request of length 2048.
All inputs are finite; a program needn't handle non-finite values.
Results may differ from the reference program's by a relative error of at most 0.018.
Values may be sent and summed in bfloat16 or wider, within the bound.
A program may use at most 64 MiB of HBM per device.

```python
import math
import jax
import jax.numpy as jnp
import numpy as np
from jax import lax

D = 3584
H = 64
LAT = 512
ROPE = 64
V = 128
FF = 2048
MB = 2
QK = 576
CTX = 2048
TOKG = 32
REQS = 128
EXPERTS = 32
TOPK = 8
CAP = 16


def draw_queries(key, part):
    key = jax.random.fold_in(key, 7)
    shape = (MB, REQS, H, QK)
    return jax.random.truncated_normal(key, -4.0, 4.0, shape, jnp.float32).astype(jnp.bfloat16)


def draw_cache(key, part):
    key = jax.random.fold_in(key, 9)
    shape = (MB, REQS, CTX, QK)
    return jax.random.truncated_normal(key, -4.0, 4.0, shape, jnp.float32).astype(jnp.bfloat16)


def draw_lengths(key, part):
    key = jax.random.fold_in(key, 13)
    drawn = jax.random.randint(key, (MB, REQS), 2, CTX + 1)
    chosen = jax.random.randint(jax.random.fold_in(key, 14), (MB, 1), 0, REQS)
    return jnp.where(jnp.arange(REQS)[None, :] == chosen, CTX, drawn).astype(jnp.int32)


def draw_resid(key, part):
    key = jax.random.fold_in(key, 17)
    column_scale = jnp.exp(jax.random.uniform(jax.random.fold_in(key, 1), (D,), jnp.float32, math.log(0.3), math.log(3.0)))
    row_scale = jnp.exp(jax.random.uniform(jax.random.fold_in(key, 2), (MB, REQS, 1), jnp.float32, math.log(0.3), math.log(3.0)))
    noise = jax.random.truncated_normal(key, -4.0, 4.0, (MB, REQS, D), jnp.float32)
    return (noise * column_scale * row_scale).astype(jnp.bfloat16)


def block_levels(key, dims, split, least, top_value):
    def one(position, blocks):
        heights = jax.random.uniform(jax.random.fold_in(jax.random.fold_in(key, 6), position), (blocks,), jnp.float32, least / len(split), top_value / len(split))
        return jnp.repeat(jnp.exp(heights), dims[position] // blocks).reshape((-1,) + (1,) * (len(dims) - position - 1))

    gain = one(*split[0])
    for cut in split[1:]:
        gain = gain * one(*cut)
    return gain


def deal_out(stream_key, own, number, rows, count, top, bound, skew):
    sequence = jax.random.permutation(stream_key, count)
    packed, usual = load_shares(count, rows * top, bound, skew, True), load_shares(count, rows * top, bound, skew, False)
    places = jnp.arange(count)

    def named(sizes, offset_by):
        used = int((sizes > 0).sum())
        fixed = max(1, used // 4)
        shifted = fixed + (places - fixed + offset_by * (used - fixed)) % max(1, count - fixed)
        return jnp.zeros((count,), jnp.int32).at[sequence[jnp.where(places < fixed, places, shifted)]].set(jnp.asarray(sizes, jnp.int32))

    sizes = jnp.where(number % 4 == 0, named(packed, number // 4), named(usual, number - number // 4 - 1))
    mixed = jax.random.permutation(jax.random.fold_in(own, 3), count)
    source_of, sink = mixed[0:count // 2 * 2:2], mixed[1:count // 2 * 2:2]
    room = jnp.minimum(sizes[source_of] - 1, bound - sizes[sink]) // 2
    room = jnp.where((source_of == sequence[0]) | (sink == sequence[0]) | (sizes[sink] == 0), 0, jnp.maximum(room, 0))
    shifted = jax.random.randint(jax.random.fold_in(own, 4), (count // 2,), 0, 1 << 20) % (room + 1)
    sizes = sizes.at[source_of].add(-shifted).at[sink].add(shifted)
    labels = jnp.searchsorted(jnp.cumsum(sizes), jnp.arange(rows * top), side="right").astype(jnp.int32)
    table = labels.reshape(top, rows).T
    table = table[jax.random.permutation(jax.random.fold_in(own, 1), rows)]
    offset_by = jax.random.randint(jax.random.fold_in(own, 2), (rows, 1), 0, top)
    return jnp.take_along_axis(table, (jnp.arange(top)[None, :] + offset_by) % top, axis=1)


def load_shares(count, total, bound, skew, full):
    loads = [(1 << 20) // math.isqrt(standing ** skew) + 1 for standing in range(1, count + 1)]
    largest = bound if full else min(bound, max(-(-total // count), total * loads[0] // sum(loads)))
    least = 1 if total - largest >= count - 1 else 0
    counts, rest = [largest] + [least] * (count - 1), total - largest - least * (count - 1)
    while rest > 0:
        candidates = [i for i in range(1, count) if counts[i] < largest] or [i for i in range(1, count) if counts[i] < bound]
        pool, remaining = sum([loads[i] for i in candidates]), rest
        for i in candidates:
            more = min(bound - counts[i], max(1, remaining * loads[i] // pool), rest)
            counts[i] = counts[i] + more
            rest = rest - more
    return np.array(counts)


def bell_draw(stream_key, shape, width, limit, pieces=(), held_as=jnp.bfloat16):
    values = jax.random.normal(stream_key, shape, jnp.float32) * width
    if len(pieces) > 0:
        values = block_levels(stream_key, shape, pieces, -0.22, 0.18) * values
    return jnp.clip(values, min=-limit, max=limit).astype(held_as)


def setup_inputs(seed: int = 0) -> dict:
    key_list = jax.random.split(jax.random.key(seed), 13)
    resid = draw_resid(jax.random.fold_in(key_list[12], 71), 0)
    queries = draw_queries(jax.random.fold_in(key_list[12], 71), 0)
    cache = draw_cache(jax.random.fold_in(key_list[12], 71), 0)
    lengths = draw_lengths(jax.random.fold_in(key_list[12], 71), 0)
    w_value = bell_draw(key_list[4], (H, LAT, V), (max(1, LAT // 64)) ** -0.5, 2.0, ((0, 32), (2, 4)))
    w_out = bell_draw(key_list[5], (H, V, D), (H * V) ** -0.5, 0.0625, ((0, 32), (1, 4)))
    norm_gain = jnp.clip(1.0 + 0.18 * jax.random.normal(key_list[6], (D,), jnp.float32), 0.099609375, 1.8984375).astype(jnp.bfloat16)
    route_ids_keys = jax.random.split(jax.random.fold_in(key_list[7], 1), MB * REQS // TOKG)
    route_ids_turns = jax.random.permutation(jax.random.fold_in(key_list[7], 3), MB * REQS // TOKG)
    route_ids = jax.vmap(lambda own, number: deal_out(jax.random.fold_in(key_list[7], 2), own, number, TOKG, EXPERTS, TOPK, CAP, 2))(route_ids_keys, route_ids_turns).reshape((MB, REQS, TOPK))
    route_weights = jnp.clip(jnp.exp(jax.random.uniform(key_list[8], (MB, REQS, TOPK), jnp.float32, math.log(0.05), math.log(1.0))), 0.05, 1.0)
    w_gate = bell_draw(key_list[9], (EXPERTS, D, FF), D ** -0.5, 0.09375, ((0, 32), (2, 16)))
    w_up = bell_draw(key_list[10], (EXPERTS, D, FF), D ** -0.5, 0.09375, ((0, 32), (2, 16)))
    w_down = bell_draw(key_list[11], (EXPERTS, FF, D), FF ** -0.5, 0.125, ((0, 32), (1, 16)))
    return {"resid": resid, "queries": queries, "cache": cache, "lengths": lengths, "w_value": w_value, "w_out": w_out, "norm_gain": norm_gain, "route_ids": route_ids, "route_weights": route_weights, "w_gate": w_gate, "w_up": w_up, "w_down": w_down}


def normalize(hidden, norm_gain):
    mean_square = lax.optimization_barrier(jnp.mean(hidden * hidden, axis=-1, keepdims=True))
    return hidden * lax.rsqrt(mean_square + 1e-06) * norm_gain.astype(jnp.float32)

def attend_request(parts):
    query_rows, key_rows, length = parts
    score_scale = (V + ROPE) ** (-0.5)
    scores = jnp.dot(query_rows, key_rows.T, preferred_element_type=jnp.float32) * score_scale
    positions = jnp.arange(CTX, dtype=jnp.int32)
    visible = (positions < length)[None, :]
    row_top = lax.optimization_barrier(jnp.max(jnp.where(visible, scores, -1e+30), axis=1, keepdims=True))
    soft_weights = jnp.where(visible, jnp.exp(scores - row_top), 0.0)
    row_total = lax.optimization_barrier(jnp.sum(soft_weights, axis=1, keepdims=True))
    summed = jnp.dot(soft_weights.astype(jnp.bfloat16), key_rows[:, :LAT], preferred_element_type=jnp.float32)
    return (summed / row_total).astype(jnp.bfloat16)

def reference(resid, queries, cache, lengths, w_value, w_out, norm_gain, route_ids, route_weights, w_gate, w_up, w_down):
    value_table = w_value.astype(jnp.float32)
    out_table = w_out.astype(jnp.float32)
    expert_ids = jnp.arange(EXPERTS, dtype=jnp.int32)
    results = []
    for micro_idx in range(MB):
        context = lax.map(attend_request, (queries[micro_idx], cache[micro_idx], lengths[micro_idx]))
        values = jnp.einsum('rhl,hlv->rhv', context.astype(jnp.float32), value_table).astype(jnp.bfloat16)
        attended = jnp.einsum('rhv,hvd->rd', values.astype(jnp.float32), out_table)
        hidden = resid[micro_idx].astype(jnp.float32) + attended
        normed = normalize(hidden, norm_gain).astype(jnp.bfloat16)
        matches = route_ids[micro_idx][:, :, None] == expert_ids[None, None, :]
        combine_table = lax.optimization_barrier(jnp.sum(jnp.where(matches, route_weights[micro_idx][:, :, None], 0.0), axis=1))

        def add_expert(running, expert_part):
            gate_part, up_part, down_part, column = expert_part
            gate_proj = jnp.dot(normed, gate_part, preferred_element_type=jnp.float32)
            up_proj = jnp.dot(normed, up_part, preferred_element_type=jnp.float32)
            activation = (jax.nn.silu(gate_proj) * up_proj).astype(jnp.bfloat16)
            expert_out = jnp.dot(activation, down_part, preferred_element_type=jnp.float32)
            return (running + column[:, None] * expert_out, None)
        mixed, unused = lax.scan(add_expert, jnp.zeros(hidden.shape, jnp.float32), (w_gate, w_up, w_down, combine_table.T))
        results.append((hidden + mixed).astype(jnp.bfloat16))
    return jnp.stack(results)
```

```python
import jax
import jax.numpy as jnp
from jax import lax
from jax.experimental import pallas as pl
from jax.experimental.pallas import tpu as pltpu
from jax.sharding import PartitionSpec as P

MESH = pl.DeviceIdType.MESH
F32 = jnp.float32
BF16 = jnp.bfloat16
SCALE = (128 + 64) ** -0.5
NT = (((1,), (1,)), ((), ()))


def remote(src, dst, send_sem, recv_sem, device):
    return pltpu.make_async_remote_copy(
        src_ref=src,
        dst_ref=dst,
        send_sem=send_sem,
        recv_sem=recv_sem,
        device_id=device,
        device_id_type=MESH,
    )


class Sends:
    def __init__(self, sems):
        self.sems = sems
        self.used = 0
        self.pending = []

    def go(self, src, dst, recv_sem, device, *conds):
        copy = remote(src, dst, self.sems.at[self.used], recv_sem, device)
        self.used += 1
        cond = None
        for item in conds:
            cond = item if cond is None else cond & item
        if cond is None:
            copy.start()
        else:
            pl.when(cond)(copy.start)
        self.pending.append((cond, copy))

    def drain(self):
        for cond, copy in self.pending:
            if cond is None:
                copy.wait_send()
            else:
                pl.when(cond)(copy.wait_send)
        self.pending = []


SEND_SEMS = 140


def kernel(
    len_ref,
    gain_ref,
    q_hbm,
    cache_hbm,
    resid_hbm,
    ids_hbm,
    wts_hbm,
    wv_hbm,
    wo_hbm,
    wg_hbm,
    wu_hbm,
    wd_hbm,
    out_ref,
    q_v,
    cache_v,
    res_v,
    ids_v,
    wts_v,
    wv_v,
    wvt_v,
    wo_v,
    wgu_v,
    wd_v,
    rw_v,
    s1_v,
    p1_v,
    c32_v,
    s2_v,
    p2_v,
    c2_v,
    s3_v,
    p3_v,
    hid_v,
    ag_v,
    pd_v,
    r0_v,
    qs_v,
    r1x_v,
    r1y_v,
    r1z_v,
    s1x_v,
    s1y_v,
    s1z_v,
    r2x_v,
    r2y_v,
    r2z_v,
    s2x_v,
    s2y_v,
    s2z_v,
    r3_v,
    f_v,
    o_v,
    lsem,
    send_sems,
    loop_sems,
    wsem,
    p1_sem,
    big_sem,
    g_sem,
    core_sem,
    r_sem,
):
    a = lax.axis_index("attn")
    g = lax.axis_index("grp")
    e = lax.axis_index("exp")
    c = e % 2
    y = (e // 2) % 8
    l = e // 16
    z = 2 * g + l
    yc = jnp.minimum(y, 6)
    has_tile = y < 7
    even = l == 0
    odd = l == 1
    first = c == 0
    second = c == 1
    sends = Sends(send_sems)
    when = pl.when

    def xi(d):
        return (a + d + 4) % 4

    def yi(d):
        return (y + d + 8) % 8

    def zi(d):
        return (z + d + 8) % 8

    def xdev(d):
        return {"attn": xi(d)}

    def ydev(d):
        return {"exp": l * 16 + yi(d) * 2 + c}

    def zdev(d):
        return {"grp": zi(d) // 2, "exp": (zi(d) % 2) * 16 + y * 2 + c}

    core_dev = {"exp": e + 1 - 2 * c}

    def arrived(dst, sem):
        remote(dst, dst, send_sems.at[0], sem, core_dev).wait_recv()

    chunk = pl.multiple_of((a * 7 + yc) * 128, 128)
    loads = [
        pltpu.make_async_copy(src, dst, lsem.at[i])
        for i, (src, dst) in enumerate(
            [
                (q_hbm, q_v),
                (cache_hbm, cache_v),
                (wv_hbm, wv_v),
                (
                    resid_hbm.at[l, pl.ds(pl.multiple_of(c * 16, 16), 16), pl.ds(chunk, 128)],
                    res_v,
                ),
                (ids_hbm, ids_v),
                (wts_hbm, wts_v),
                (
                    wo_hbm.at[:, :, pl.ds(pl.multiple_of(a * 896, 128), 896)],
                    wo_v.at[a],
                ),
                (wg_hbm, wgu_v.at[:, pl.ds(0, 128)]),
                (wu_hbm, wgu_v.at[:, pl.ds(128, 128)]),
                (wd_hbm, wd_v),
            ]
        )
    ]
    for load in loads:
        load.start()

    barrier = pltpu.get_barrier_semaphore()

    def greet(device):
        pl.semaphore_signal(barrier, inc=1, device_id=device, device_id_type=MESH)

    for d in range(1, 4):
        greet(xdev(d))
    for d in range(1, 8):
        greet(zdev(d))

    def greet_plane(i, carry):
        greet({"exp": (e + i) % 32})
        return carry

    lax.fori_loop(1, 32, greet_plane, 0)
    pl.semaphore_wait(barrier, 41)

    loads[0].wait()
    loads[1].wait()
    row = lax.broadcasted_iota(jnp.int32, (64, 64), 0)
    col = lax.broadcasted_iota(jnp.int32, (64, 64), 1)
    head = ((row & 15) >> 1) * 8 + (row >> 4) * 2 + (row & 1)
    perm = jnp.where(head == col, 1.0, 0.0).astype(BF16)
    pos = a * 512 + lax.broadcasted_iota(jnp.int32, (64, 512), 1)
    lane = lax.broadcasted_iota(jnp.int32, (64, 128), 1)
    for mb in range(2):
        qp = jnp.dot(perm, q_v[mb], preferred_element_type=F32).astype(BF16)
        scores = lax.dot_general(qp, cache_v[mb], NT, preferred_element_type=F32) * SCALE
        visible = pos < len_ref[mb, 0]
        top = jnp.max(jnp.where(visible, scores, -1e30), axis=1, keepdims=True)
        top = top.astype(BF16).astype(F32)
        weights = jnp.where(visible, jnp.exp(scores - top), 0.0)
        total = jnp.sum(weights, axis=1, keepdims=True)
        acc = jnp.dot(weights.astype(BF16), cache_v[mb, :, 0:512], preferred_element_type=F32)
        hi = total.astype(BF16).astype(F32)
        stats = jnp.where(lane == 0, top, jnp.where(lane == 1, hi, total - hi))
        s1_v[:, mb, :, 0:512] = acc.astype(BF16).reshape(4, 16, 512)
        s1_v[:, mb, :, 512:640] = stats.astype(BF16).reshape(4, 16, 128)
    for d in range(1, 4):
        sends.go(s1_v.at[xi(d)], p1_v.at[d - 1], p1_sem.at[d - 1], xdev(d))

    loads[2].wait()
    eye = jnp.where(
        lax.broadcasted_iota(jnp.int32, (32, 32), 0)
        == lax.broadcasted_iota(jnp.int32, (32, 32), 1),
        1.0,
        0.0,
    ).astype(BF16)
    for h in range(2):
        wvt_v[a, h] = lax.dot_general(eye, wv_v[h], NT, preferred_element_type=F32).astype(BF16)
    for d in range(1, 4):
        sends.go(wvt_v.at[a], wvt_v.at[a], wsem.at[d - 1], xdev(d))
        sends.go(
            wo_hbm.at[:, :, pl.ds(pl.multiple_of(xi(d) * 896, 128), 896)],
            wo_v.at[a],
            wsem.at[2 + d],
            xdev(d),
        )

    loads[4].wait()
    loads[5].wait()
    for mb in range(2):
        gate = jnp.sum(
            jnp.where(ids_v[mb] == e, wts_v[mb], 0.0), axis=1, keepdims=True
        )
        gate = jnp.broadcast_to(gate, (128, 128))
        for grp in range(4):
            at = (grp * 2 + mb) * 32
            rw_v[at : at + 32, :] = gate[grp * 32 : (grp + 1) * 32, :]

    for d in range(1, 4):
        arrived(p1_v.at[d - 1], p1_sem.at[d - 1])
    blocks = [s1_v[a]] + [p1_v[d] for d in range(3)]
    blocks = [b.astype(F32).reshape(32, 640) for b in blocks]
    tops = [b[:, 512:513] for b in blocks]
    row_top = jnp.maximum(jnp.maximum(tops[0], tops[1]), jnp.maximum(tops[2], tops[3]))
    ctx_sum = jnp.zeros((32, 512), F32)
    row_total = jnp.zeros((32, 1), F32)
    for b, t in zip(blocks, tops):
        factor = jnp.exp(t - row_top)
        ctx_sum = ctx_sum + b[:, 0:512] * factor
        row_total = row_total + (b[:, 513:514] + b[:, 514:515]) * factor
    context = ctx_sum / row_total
    for mb in range(2):
        for k in range(4):
            c32_v[:, mb * 4 + k, :] = context[
                mb * 16 : (mb + 1) * 16, k * 128 : (k + 1) * 128
            ]
    s2_v[...] = c32_v[...].reshape(8, 16, 128).astype(BF16)

    def p2_copy(i):
        j = (i // 4 + e) % 8
        to_a = (a + i) % 4
        to_e = 4 * j + a
        mine = (to_a == a) & (to_e == e)
        far = remote(
            s2_v.at[j],
            p2_v.at[e],
            loop_sems.at[i],
            big_sem.at[0],
            {"attn": to_a, "exp": to_e},
        )
        near = pltpu.make_async_copy(s2_v.at[j], p2_v.at[e], big_sem.at[0])
        return mine, far, near

    def p2_go(i, carry):
        mine, far, near = p2_copy(i)
        pl.when(mine)(near.start)
        pl.when(jnp.logical_not(mine))(far.start)
        return carry

    def p2_done(i, carry):
        mine, far, near = p2_copy(i)
        pl.when(jnp.logical_not(mine))(far.wait_send)
        return carry

    lax.fori_loop(0, 32, p2_go, 0)

    loads[6].wait()
    for d in range(1, 4):
        arrived(wvt_v.at[xi(-d)], wsem.at[d - 1])
        arrived(wo_v.at[xi(-d)], wsem.at[2 + d])
    pltpu.make_async_copy(p2_v, p2_v, big_sem.at[0]).wait()
    c2_v[...] = p2_v[...].astype(F32)
    out = jnp.zeros((64, 896), F32)
    for h in range(2):
        rows = [
            jnp.concatenate([c2_v[:, h * 8 + mb * 4 + k, :] for k in range(4)], axis=1)
            for mb in range(2)
        ]
        ctx = jnp.concatenate(rows, axis=0).astype(BF16)
        values = lax.dot_general(
            ctx, wvt_v[:, h].reshape(128, 512), NT, preferred_element_type=F32
        ).astype(BF16)
        out = out + jnp.dot(
            values, wo_v[:, h].reshape(128, 896), preferred_element_type=F32
        )
    for k in range(7):
        s3_v[k] = out[:, k * 128 : (k + 1) * 128].astype(BF16).reshape(4, 16, 128)

    def p3_copy(i):
        to_e = (e + i) % 32
        to_y = (to_e // 2) % 8
        tile = (to_e // 16) * 2 + to_e % 2
        src = s3_v.at[jnp.minimum(to_y, 6), tile]
        far = remote(src, p3_v.at[e], loop_sems.at[32 + i], big_sem.at[1], {"exp": to_e})
        return to_y < 7, far

    def p3_go(i, carry):
        used, far = p3_copy(i)
        pl.when(used)(far.start)
        return carry

    def p3_done(i, carry):
        used, far = p3_copy(i)
        pl.when(used)(far.wait_send)
        return carry

    lax.fori_loop(1, 32, p3_go, 0)

    @when(has_tile)
    def _():
        pltpu.make_async_copy(s3_v.at[yc, l * 2 + c], p3_v.at[e], big_sem.at[1]).start()
        loads[3].wait()
        pltpu.make_async_copy(p3_v, p3_v, big_sem.at[1]).wait()
        attended = jnp.sum(p3_v[...].astype(F32), axis=0)
        hidden = res_v[...].astype(F32) + attended
        hid_v[...] = hidden
        ag_v[a, yc, g, l, c] = (hidden * gain_ref[pl.ds(a * 7 + yc, 1), :]).astype(BF16)

    @when(jnp.logical_not(has_tile))
    def _():
        loads[3].wait()

    own = ag_v.at[a, yc, g, l, c]
    for d in range(1, 8):
        sends.go(own, own, g_sem.at[d - 1], ydev(d), even, has_tile)
    for d in range(1, 8):
        sends.go(own, own, g_sem.at[7 + d - 1], zdev(d), odd, first, has_tile)
    for d in range(1, 4):
        sends.go(own, own, g_sem.at[14 + d - 1], xdev(d), odd, second, has_tile)

    @when(even)
    def _():
        for d in range(1, 8):

            @when(yi(-d) < 7)
            def _():
                arrived(ag_v.at[a, jnp.minimum(yi(-d), 6), g, 0, c], g_sem.at[d - 1])

    for d in range(1, 8):
        blk = ag_v.at[a, :, g, 0, c]
        sends.go(blk, blk, g_sem.at[17 + d - 1], zdev(d), even)

    @when(first & has_tile)
    def _():
        for d in range(1, 8):

            @when(zi(-d) % 2 == 1)
            def _():
                arrived(ag_v.at[a, yc, zi(-d) // 2, 1, 0], g_sem.at[7 + d - 1])

    for d in range(1, 4):
        blk = ag_v.at[a, yc, :, 1, 0]
        sends.go(blk, blk, g_sem.at[24 + d - 1], xdev(d), first, has_tile)

    @when(odd & second & has_tile)
    def _():
        for d in range(1, 4):
            arrived(ag_v.at[xi(-d), yc, g, 1, 1], g_sem.at[14 + d - 1])

    for d in range(1, 8):
        blk = ag_v.at[:, yc, g, 1, 1]
        sends.go(blk, blk, g_sem.at[27 + d - 1], ydev(d), odd, second, has_tile)

    for d in range(1, 8):

        @when(zi(-d) % 2 == 0)
        def _():
            arrived(ag_v.at[a, :, zi(-d) // 2, 0, c], g_sem.at[17 + d - 1])

    blk_x = ag_v.at[a, :, :, 0, c]
    for d in range(1, 4):
        sends.go(blk_x, blk_x, g_sem.at[34 + d - 1], xdev(d))
    sends.go(blk_x, blk_x, core_sem.at[0], core_dev)

    @when(first & has_tile)
    def _():
        for d in range(1, 4):
            arrived(ag_v.at[xi(-d), yc, :, 1, 0], g_sem.at[24 + d - 1])

    blk_y = ag_v.at[:, yc, :, 1, 0]
    for d in range(1, 8):
        sends.go(blk_y, blk_y, g_sem.at[37 + d - 1], ydev(d), first, has_tile)
    sends.go(blk_y, blk_y, core_sem.at[4], core_dev, first, has_tile)

    @when(odd & second)
    def _():
        for d in range(1, 8):

            @when(yi(-d) < 7)
            def _():
                arrived(ag_v.at[:, jnp.minimum(yi(-d), 6), g, 1, 1], g_sem.at[27 + d - 1])

    blk_z = ag_v.at[:, :, g, 1, 1]
    for d in range(1, 8):
        sends.go(blk_z, blk_z, g_sem.at[44 + d - 1], zdev(d), odd, second)
    sends.go(blk_z, blk_z, core_sem.at[12], core_dev, odd, second)

    for d in range(1, 4):
        blk = ag_v.at[xi(-d), :, :, 0, c]
        arrived(blk, g_sem.at[34 + d - 1])
        sends.go(blk, blk, core_sem.at[d], core_dev)
    for d in range(1, 8):
        cond = first & (yi(-d) < 7)
        blk = ag_v.at[:, jnp.minimum(yi(-d), 6), :, 1, 0]

        @when(cond)
        def _():
            arrived(blk, g_sem.at[37 + d - 1])

        sends.go(blk, blk, core_sem.at[4 + d], core_dev, cond)
    for d in range(1, 8):
        cond = second & (zi(-d) % 2 == 1)
        blk = ag_v.at[:, :, zi(-d) // 2, 1, 1]

        @when(cond)
        def _():
            arrived(blk, g_sem.at[44 + d - 1])

        sends.go(blk, blk, core_sem.at[12 + d], core_dev, cond)
    for d in range(4):
        arrived(ag_v.at[xi(-d), :, :, 0, 1 - c], core_sem.at[d])
    for d in range(8):

        @when(second & (yi(-d) < 7))
        def _():
            arrived(ag_v.at[:, jnp.minimum(yi(-d), 6), :, 1, 0], core_sem.at[4 + d])

        @when(first & (zi(-d) % 2 == 1))
        def _():
            arrived(ag_v.at[:, :, zi(-d) // 2, 1, 1], core_sem.at[12 + d])

    loads[7].wait()
    loads[8].wait()
    loads[9].wait()
    pieces = [ag_v[i // 7, i % 7].reshape(256, 128) for i in range(28)]
    square = jnp.zeros((256, 128), F32)
    for i in range(28):
        item = pieces[i].astype(F32) / gain_ref[i : i + 1, :]
        square = square + item * item
    inverse = lax.rsqrt(jnp.sum(square, axis=1, keepdims=True) * (1.0 / 3584) + 1e-6)
    both = jnp.dot(jnp.concatenate(pieces, axis=1), wgu_v[...], preferred_element_type=F32)
    both = both * inverse
    gate = both[:, 0:128]
    act = gate / (1.0 + jnp.exp(-gate)) * both[:, 128:256] * rw_v[...]
    act = act.astype(BF16)
    for d in (1, 2, 3, 0):
        x = xi(d)
        down = jnp.dot(
            act,
            wd_v[:, pl.ds(pl.multiple_of(x * 896, 128), 896)],
            preferred_element_type=F32,
        )
        for k in range(7):
            pd_v[x, k] = (
                down[:, k * 128 : (k + 1) * 128].astype(BF16).reshape(4, 2, 2, 16, 128)
            )
        sends.go(pd_v.at[x, :, :, :, 1 - c], r0_v.at[x], r_sem.at[d], core_dev)

    for d in (1, 2, 3, 0):
        x = xi(d)
        arrived(r0_v.at[x], r_sem.at[d])
        qs_v[x] = (pd_v[x, :, :, :, c].astype(F32) + r0_v[x].astype(F32)).astype(BF16)
        if d > 0:
            sends.go(qs_v.at[x, :, :, 0], r1x_v.at[d - 1], r_sem.at[4 + d - 1], xdev(d))
    for d in range(1, 8):
        sends.go(
            qs_v.at[:, jnp.minimum(yi(d), 6), :, 1],
            r1y_v.at[d - 1],
            r_sem.at[7 + d - 1],
            ydev(d),
            first,
            yi(d) < 7,
        )
    for d in range(1, 8):
        sends.go(
            qs_v.at[:, :, zi(d) // 2, 1],
            r1z_v.at[d - 1],
            r_sem.at[14 + d - 1],
            zdev(d),
            second,
            zi(d) % 2 == 1,
        )

    def total_of(own_block, ref, count):
        result = own_block.astype(F32)
        for i in range(count):
            result = result + ref[i].astype(F32)
        return result

    def all_arrived(ref, base, count):
        for i in range(count):
            arrived(ref.at[i], r_sem.at[base + i])

    all_arrived(r1x_v, 4, 3)
    s1x_v[...] = total_of(qs_v[a, :, :, 0], r1x_v, 3).astype(BF16)
    for d in range(1, 8):
        sends.go(
            s1x_v.at[:, zi(d) // 2],
            r2x_v.at[d - 1],
            r_sem.at[21 + d - 1],
            zdev(d),
            zi(d) % 2 == 0,
        )

    @when(first & has_tile)
    def _():
        all_arrived(r1y_v, 7, 7)
        s1y_v[...] = total_of(qs_v[:, yc, :, 1], r1y_v, 7).astype(BF16)

    for d in range(1, 4):
        sends.go(
            s1y_v.at[xi(d)],
            r2y_v.at[d - 1],
            r_sem.at[28 + d - 1],
            xdev(d),
            first,
            has_tile,
        )

    @when(second & odd)
    def _():
        all_arrived(r1z_v, 14, 7)
        s1z_v[...] = total_of(qs_v[:, :, g, 1], r1z_v, 7).astype(BF16)

    for d in range(1, 8):
        sends.go(
            s1z_v.at[:, jnp.minimum(yi(d), 6)],
            r2z_v.at[d - 1],
            r_sem.at[31 + d - 1],
            ydev(d),
            second,
            odd,
            yi(d) < 7,
        )

    @when(even)
    def _():
        all_arrived(r2x_v, 21, 7)
        s2x_v[...] = total_of(s1x_v[:, g], r2x_v, 7).astype(BF16)

    for d in range(1, 8):
        sends.go(
            s2x_v.at[jnp.minimum(yi(d), 6)],
            r3_v.at[d - 1],
            r_sem.at[38 + d - 1],
            ydev(d),
            even,
            yi(d) < 7,
        )

    @when(first & has_tile)
    def _():
        all_arrived(r2y_v, 28, 3)
        s2y_v[...] = total_of(s1y_v[a], r2y_v, 3).astype(BF16)

    for d in range(1, 8):
        sends.go(
            s2y_v.at[zi(d) // 2],
            r3_v.at[d - 1],
            r_sem.at[38 + d - 1],
            zdev(d),
            first,
            has_tile,
            zi(d) % 2 == 1,
        )

    @when(second & odd & has_tile)
    def _():
        all_arrived(r2z_v, 31, 7)
        s2z_v[...] = total_of(s1z_v[:, yc], r2z_v, 7).astype(BF16)

    for d in range(1, 4):
        sends.go(
            s2z_v.at[xi(d)],
            r3_v.at[d - 1],
            r_sem.at[38 + d - 1],
            xdev(d),
            second,
            odd,
            has_tile,
        )

    def put_rows(tile):
        for i in range(16):
            f_v[i] = tile[i : i + 1, :]

    @when(even & has_tile)
    def _():
        all_arrived(r3_v, 38, 7)
        put_rows(hid_v[...] + total_of(s2x_v[yc], r3_v, 7))

    @when(odd & first & has_tile)
    def _():
        all_arrived(r3_v, 38, 7)
        put_rows(hid_v[...] + total_of(s2y_v[g], r3_v, 7))

    @when(odd & second & has_tile)
    def _():
        all_arrived(r3_v, 38, 3)
        put_rows(hid_v[...] + total_of(s2z_v[a], r3_v, 3))

    def last_copy(i):
        to_e = c * 16 + i
        far = remote(
            f_v.at[i], o_v.at[l, yc], loop_sems.at[64 + i], big_sem.at[2], {"exp": to_e}
        )
        near = pltpu.make_async_copy(f_v.at[i], o_v.at[l, yc], big_sem.at[2])
        return to_e == e, far, near

    def last_go(i, carry):
        mine, far, near = last_copy(i)
        pl.when(mine)(near.start)
        pl.when(jnp.logical_not(mine))(far.start)
        return carry

    def last_done(i, carry):
        mine, far, near = last_copy(i)
        pl.when(jnp.logical_not(mine))(far.wait_send)
        return carry

    @when(has_tile)
    def _():
        lax.fori_loop(0, 16, last_go, 0)

    lax.fori_loop(0, 32, p2_done, 0)
    lax.fori_loop(1, 32, p3_done, 0)
    sends.drain()

    @when(has_tile)
    def _():
        lax.fori_loop(0, 16, last_done, 0)

    pltpu.make_async_copy(o_v, o_v, big_sem.at[2]).wait()
    for mb in range(2):
        out_ref[mb] = jnp.concatenate([o_v[mb, k] for k in range(7)], axis=1).astype(BF16)


def body(
    resid,
    queries,
    cache,
    lengths,
    w_value,
    w_out,
    norm_gain,
    route_ids,
    route_weights,
    w_gate,
    w_up,
    w_down,
):
    hbm = pl.BlockSpec(memory_space=pl.ANY)
    vmem = pl.BlockSpec(memory_space=pltpu.VMEM)
    smem = pl.BlockSpec(memory_space=pltpu.SMEM)

    def bf(*shape):
        return pltpu.VMEM(shape, BF16)

    def f32(*shape):
        return pltpu.VMEM(shape, F32)

    def dma(count):
        return pltpu.SemaphoreType.DMA((count,))

    return pl.pallas_call(
        kernel,
        out_shape=jax.ShapeDtypeStruct((2, 1, 896), BF16),
        in_specs=[smem, vmem] + [hbm] * 10,
        out_specs=vmem,
        scratch_shapes=[
            bf(2, 64, 576),
            bf(2, 512, 576),
            bf(16, 128),
            pltpu.VMEM((2, 128, 8), jnp.int32),
            f32(2, 128, 8),
            bf(2, 512, 32),
            bf(4, 2, 32, 512),
            bf(4, 2, 32, 896),
            bf(3584, 256),
            bf(128, 3584),
            f32(256, 128),
            bf(4, 2, 16, 640),
            bf(3, 2, 16, 640),
            f32(16, 8, 128),
            bf(8, 16, 128),
            bf(32, 16, 128),
            f32(32, 16, 128),
            bf(7, 4, 16, 128),
            bf(32, 16, 128),
            f32(16, 128),
            bf(4, 7, 4, 2, 2, 16, 128),
            bf(4, 7, 4, 2, 2, 16, 128),
            bf(4, 7, 4, 2, 16, 128),
            bf(4, 7, 4, 2, 16, 128),
            bf(3, 7, 4, 16, 128),
            bf(7, 4, 4, 16, 128),
            bf(7, 4, 7, 16, 128),
            bf(7, 4, 16, 128),
            bf(4, 4, 16, 128),
            bf(4, 7, 16, 128),
            bf(7, 7, 16, 128),
            bf(3, 4, 16, 128),
            bf(7, 4, 16, 128),
            bf(7, 16, 128),
            bf(4, 16, 128),
            bf(4, 16, 128),
            bf(7, 16, 128),
            f32(16, 1, 128),
            f32(2, 7, 1, 128),
            dma(10),
            dma(SEND_SEMS),
            dma(80),
            dma(6),
            dma(3),
            dma(3),
            dma(51),
            dma(20),
            dma(45),
        ],
        compiler_params=pltpu.CompilerParams(
            collective_id=0, has_side_effects=True, vmem_limit_bytes=56 * 1024 * 1024
        ),
        name="layer",
    )(
        lengths,
        norm_gain.astype(F32).reshape(28, 128),
        queries[:, 0],
        cache[:, 0],
        resid,
        route_ids,
        route_weights,
        w_value,
        w_out,
        w_gate[0],
        w_up[0],
        w_down[0],
    )


def solution(mesh):
    return jax.shard_map(
        body,
        mesh=mesh,
        in_specs=(
            P(None, "grp", None),
            P(None, ("grp", "exp"), None, None),
            P(None, ("grp", "exp"), "attn", None),
            P(None, ("grp", "exp")),
            P("exp", None, "attn"),
            P("exp", "attn", None),
            P(),
            P(),
            P(),
            P("exp", None, ("attn", "grp")),
            P("exp", None, ("attn", "grp")),
            P("exp", ("attn", "grp"), None),
        ),
        out_specs=P(None, ("grp", "exp"), "attn"),
        check_vma=False,
    )
```

```python
import jax
import jax.numpy as jnp
from jax import lax
from jax.experimental import pallas as pl
from jax.experimental.pallas import tpu as pltpu
from jax.sharding import PartitionSpec as P

MESH = pl.DeviceIdType.MESH
F32 = jnp.float32
BF16 = jnp.bfloat16
SCALE = (128 + 64) ** -0.5
NT = (((1,), (1,)), ((), ()))


def remote(src, dst, send_sem, recv_sem, device):
    return pltpu.make_async_remote_copy(
        src_ref=src,
        dst_ref=dst,
        send_sem=send_sem,
        recv_sem=recv_sem,
        device_id=device,
        device_id_type=MESH,
    )


class Sends:
    def __init__(self, sems):
        self.sems = sems
        self.used = 0
        self.pending = []

    def go(self, src, dst, recv_sem, device, *conds):
        copy = remote(src, dst, self.sems.at[self.used], recv_sem, device)
        self.used += 1
        cond = None
        for item in conds:
            cond = item if cond is None else cond & item
        if cond is None:
            copy.start()
        else:
            pl.when(cond)(copy.start)
        self.pending.append((cond, copy))

    def drain(self):
        for cond, copy in self.pending:
            if cond is None:
                copy.wait_send()
            else:
                pl.when(cond)(copy.wait_send)
        self.pending = []


FAR8 = (4, 3, 5, 2, 6, 1, 7)
FAR4 = (2, 1, 3)
NEAR8 = (1, 7, 2, 6, 3, 5, 4)
NEAR4 = (1, 3, 2)
SEND_SEMS = 232


def kernel(
    len_ref,
    gain_ref,
    q_hbm,
    cache_hbm,
    resid_hbm,
    ids_hbm,
    wts_hbm,
    wv_hbm,
    wo_hbm,
    wg_hbm,
    wu_hbm,
    wd_hbm,
    out_ref,
    q_v,
    cache_v,
    res_v,
    ids_v,
    wts_v,
    wvt_v,
    wo_v,
    wgu_v,
    wd_v,
    rw_v,
    gain_v,
    s1_v,
    p1_v,
    c32_v,
    s2_v,
    p2_v,
    c2_v,
    s3_v,
    p3_v,
    hid_v,
    ag_v,
    pd_v,
    r0_v,
    qs_v,
    r1x_v,
    r1y_v,
    r1z_v,
    s1x_v,
    s1y_v,
    s1z_v,
    r2x_v,
    r2y_v,
    r2z_v,
    s2x_v,
    s2y_v,
    s2z_v,
    r3_v,
    f_v,
    o_v,
    unit_v,
    fin_v,
    lsem,
    send_sems,
    loop_sems,
    wsem,
    p1_sem,
    big_sem,
    g_sem,
    core_sem,
    r_sem,
):
    a = lax.axis_index("attn")
    g = lax.axis_index("grp")
    e = lax.axis_index("exp")
    c = e % 2
    y = (e // 2) % 8
    l = e // 16
    z = 2 * g + l
    yc = jnp.minimum(y, 6)
    has_tile = y < 7
    even = l == 0
    odd = l == 1
    first = c == 0
    second = c == 1
    sends = Sends(send_sems)
    when = pl.when

    def xi(d):
        return (a + d + 4) % 4

    def yi(d):
        return (y + d + 8) % 8

    def zi(d):
        return (z + d + 8) % 8

    def xdev(d):
        return {"attn": xi(d)}

    def ydev(d):
        return {"exp": l * 16 + yi(d) * 2 + c}

    def zdev(d):
        return {"grp": zi(d) // 2, "exp": (zi(d) % 2) * 16 + y * 2 + c}

    core_dev = {"exp": e + 1 - 2 * c}

    def arrived(dst, sem):
        remote(dst, dst, send_sems.at[0], sem, core_dev).wait_recv()

    chunk = pl.multiple_of((a * 7 + yc) * 128, 128)
    loads = [
        pltpu.make_async_copy(src, dst, lsem.at[i])
        for i, (src, dst) in enumerate(
            [
                (q_hbm, q_v),
                (cache_hbm, cache_v),
                (wv_hbm, wvt_v.at[a]),
                (
                    resid_hbm.at[l, pl.ds(pl.multiple_of(c * 16, 16), 16), pl.ds(chunk, 128)],
                    res_v,
                ),
                (ids_hbm, ids_v),
                (wts_hbm, wts_v),
                (
                    wo_hbm.at[:, :, pl.ds(pl.multiple_of(a * 896, 128), 896)],
                    wo_v.at[a],
                ),
                (wg_hbm, wgu_v.at[:, pl.ds(0, 128)]),
                (wu_hbm, wgu_v.at[:, pl.ds(128, 128)]),
                (wd_hbm, wd_v),
            ]
        )
    ]
    for load in loads:
        load.start()

    barrier = pltpu.get_barrier_semaphore()

    def greet(device):
        pl.semaphore_signal(barrier, inc=1, device_id=device, device_id_type=MESH)


    def greet_plane(i, carry):
        greet({"exp": (e + i) % 32})
        return carry

    lax.fori_loop(8, 32, greet_plane, 0)
    for d in FAR8:
        greet(zdev(d))
    for d in FAR4:
        greet(xdev(d))
    lax.fori_loop(1, 8, greet_plane, 0)

    gain_v[...] = gain_ref[...].astype(F32)
    unit_v[:, :, 8:16, :] = jnp.zeros((2, 128, 8, 128), F32)

    loads[0].wait()
    loads[1].wait()
    row = lax.broadcasted_iota(jnp.int32, (64, 64), 0)
    col = lax.broadcasted_iota(jnp.int32, (64, 64), 1)
    head = ((row & 15) >> 1) * 8 + (row >> 4) * 2 + (row & 1)
    perm = jnp.where(head == col, 1.0, 0.0).astype(BF16)
    pos = a * 512 + lax.broadcasted_iota(jnp.int32, (64, 512), 1)
    lane = lax.broadcasted_iota(jnp.int32, (64, 128), 1)
    for mb in range(2):
        qp = jnp.dot(perm, q_v[mb], preferred_element_type=F32).astype(BF16)
        scores = jnp.dot(qp, cache_v[mb], preferred_element_type=F32) * SCALE
        visible = pos < len_ref[0, mb]
        top = jnp.max(jnp.where(visible, scores, -1e30), axis=1, keepdims=True)
        top = top.astype(BF16).astype(F32)
        weights = jnp.where(visible, jnp.exp(scores - top), 0.0)
        total = jnp.sum(weights, axis=1, keepdims=True)
        acc = lax.dot_general(
            weights.astype(BF16), cache_v[mb, 0:512, :], NT, preferred_element_type=F32
        )
        hi = total.astype(BF16).astype(F32)
        stats = jnp.where(lane == 0, top, jnp.where(lane == 1, hi, total - hi))
        s1_v[:, mb, :, 0:512] = acc.astype(BF16).reshape(4, 16, 512)
        s1_v[:, mb, :, 512:640] = stats.astype(BF16).reshape(4, 16, 128)
    pl.semaphore_wait(barrier, 41)
    for d in FAR4:
        sends.go(s1_v.at[xi(d)], p1_v.at[d - 1], p1_sem.at[d - 1], xdev(d))

    loads[4].wait()
    loads[5].wait()
    for mb in range(2):
        gate = jnp.sum(
            jnp.where(ids_v[mb] == e, wts_v[mb], 0.0), axis=0, keepdims=True
        )
        gate = jnp.broadcast_to(gate, (128, 128)).T
        for grp in range(4):
            at = (grp * 2 + mb) * 32
            rw_v[at : at + 32, :] = gate[grp * 32 : (grp + 1) * 32, :]

    loads[2].wait()
    for d in FAR4:
        sends.go(wvt_v.at[a], wvt_v.at[a], wsem.at[d - 1], xdev(d))

    for d in range(1, 4):
        arrived(p1_v.at[d - 1], p1_sem.at[d - 1])
    blocks = [s1_v[a]] + [p1_v[d] for d in range(3)]
    blocks = [b.astype(F32).reshape(32, 640) for b in blocks]
    tops = [b[:, 512:513] for b in blocks]
    row_top = jnp.maximum(jnp.maximum(tops[0], tops[1]), jnp.maximum(tops[2], tops[3]))
    ctx_sum = jnp.zeros((32, 512), F32)
    row_total = jnp.zeros((32, 1), F32)
    for b, t in zip(blocks, tops):
        factor = jnp.exp(t - row_top)
        ctx_sum = ctx_sum + b[:, 0:512] * factor
        row_total = row_total + (b[:, 513:514] + b[:, 514:515]) * factor
    context = ctx_sum / row_total
    for mb in range(2):
        for k in range(4):
            c32_v[:, mb * 4 + k, :] = context[
                mb * 16 : (mb + 1) * 16, k * 128 : (k + 1) * 128
            ]
    s2_v[...] = c32_v[...].reshape(8, 16, 128).astype(BF16)

    for s_off in (2, 1, 3, 0):
        for d in FAR4 + (0,):
            for half in (1, 0):
                j = (half + l) % 2 * 4 + (y // 2 + s_off) % 4
                to_e = 4 * j + a
                device = {"attn": xi(d), "exp": to_e}
                if s_off == 0 and d == 0:
                    mine = to_e == e
                    near = pltpu.make_async_copy(s2_v.at[j], p2_v.at[e], big_sem.at[0])
                    when(mine)(near.start)
                    sends.go(
                        s2_v.at[j], p2_v.at[e], big_sem.at[0], device, jnp.logical_not(mine)
                    )
                else:
                    sends.go(s2_v.at[j], p2_v.at[e], big_sem.at[0], device)

    for d in FAR4:
        sends.go(
            wo_hbm.at[:, :, pl.ds(pl.multiple_of(xi(d) * 896, 128), 896)],
            wo_v.at[a],
            wsem.at[2 + d],
            xdev(d),
        )
    loads[6].wait()
    for d in range(1, 4):
        arrived(wvt_v.at[xi(-d)], wsem.at[d - 1])
        arrived(wo_v.at[xi(-d)], wsem.at[2 + d])
    pltpu.make_async_copy(p2_v, p2_v, big_sem.at[0]).wait()
    c2_v[...] = p2_v[...].astype(F32)
    out = jnp.zeros((64, 896), F32)
    for h in range(2):
        rows = [
            jnp.concatenate([c2_v[:, h * 8 + mb * 4 + k, :] for k in range(4)], axis=1)
            for mb in range(2)
        ]
        ctx = jnp.concatenate(rows, axis=0).astype(BF16)
        values = lax.dot_general(
            ctx, wvt_v[:, h].reshape(128, 512), NT, preferred_element_type=F32
        ).astype(BF16)
        out = out + jnp.dot(
            values, wo_v[:, h].reshape(128, 896), preferred_element_type=F32
        )
    for k in range(7):
        s3_v[k] = out[:, k * 128 : (k + 1) * 128].astype(BF16).reshape(4, 16, 128)

    for d in FAR8 + (0,):
        for half in (1, 0):
            for core in (1, 0):
                if d == 0 and half == 0 and core == 0:
                    continue
                to_l, to_c = (l + half) % 2, (c + core) % 2
                src = s3_v.at[jnp.minimum(yi(d), 6), to_l * 2 + to_c]
                device = {"exp": to_l * 16 + yi(d) * 2 + to_c}
                sends.go(src, p3_v.at[e], big_sem.at[1], device, yi(d) < 7)

    @when(has_tile)
    def _():
        pltpu.make_async_copy(s3_v.at[yc, l * 2 + c], p3_v.at[e], big_sem.at[1]).start()
        loads[3].wait()
        pltpu.make_async_copy(p3_v, p3_v, big_sem.at[1]).wait()
        attended = jnp.sum(p3_v[...].astype(F32), axis=0)
        hidden = res_v[...].astype(F32) + attended
        hid_v[...] = hidden
        ag_v[a, yc, g, l, c] = (hidden * gain_v[pl.ds(a * 7 + yc, 1), :]).astype(BF16)

    @when(jnp.logical_not(has_tile))
    def _():
        loads[3].wait()

    own = ag_v.at[a, yc, g, l, c]
    for d in FAR8:
        sends.go(own, own, g_sem.at[d - 1], ydev(d), even, has_tile)
    for d in FAR8:
        sends.go(own, own, g_sem.at[7 + d - 1], zdev(d), odd, first, has_tile)
    for d in FAR4:
        sends.go(own, own, g_sem.at[14 + d - 1], xdev(d), odd, second, has_tile)

    def hidden_copy(i):
        to_e = c * 16 + i
        far = remote(
            f_v.at[i], o_v.at[l, yc], loop_sems.at[i], big_sem.at[2], {"exp": to_e}
        )
        return to_e == e, far

    def hidden_go(i, carry):
        mine, far = hidden_copy(i)

        @when(mine)
        def _():
            pltpu.make_async_copy(f_v.at[i], o_v.at[l, yc], big_sem.at[2]).start()

        pl.when(jnp.logical_not(mine))(far.start)
        return carry

    def hidden_done(i, carry):
        mine, far = hidden_copy(i)
        pl.when(jnp.logical_not(mine))(far.wait_send)
        return carry

    @when(has_tile)
    def _():
        for i in range(16):
            f_v[i] = hid_v[i : i + 1, :]
        lax.fori_loop(0, 16, hidden_go, 0)

    @when(odd & second & has_tile)
    def _():
        for d in NEAR4:
            arrived(ag_v.at[xi(-d), yc, g, 1, 1], g_sem.at[14 + d - 1])

    for d in FAR8:
        blk = ag_v.at[:, yc, g, 1, 1]
        sends.go(blk, blk, g_sem.at[27 + d - 1], ydev(d), odd, second, has_tile)

    @when(even)
    def _():
        for d in NEAR8:

            @when(yi(-d) < 7)
            def _():
                arrived(ag_v.at[a, jnp.minimum(yi(-d), 6), g, 0, c], g_sem.at[d - 1])

    for d in FAR8:
        blk = ag_v.at[a, :, g, 0, c]
        sends.go(blk, blk, g_sem.at[17 + d - 1], zdev(d), even)

    @when(first & has_tile)
    def _():
        for d in NEAR8:

            @when(zi(-d) % 2 == 1)
            def _():
                arrived(ag_v.at[a, yc, zi(-d) // 2, 1, 0], g_sem.at[7 + d - 1])

    for d in FAR4:
        blk = ag_v.at[a, yc, :, 1, 0]
        sends.go(blk, blk, g_sem.at[24 + d - 1], xdev(d), first, has_tile)

    def part(p):
        offset = (0, 2, 6, 4)[p] + l * (1, 5, -3, 1)[p]
        return offset, (z - offset + 8) % 8 // 2

    def pass_on(p):
        offset, from_g = part(p)
        blk = ag_v.at[a, :, from_g, 0, c]
        if p == 0:

            @when(odd)
            def _():
                arrived(blk, g_sem.at[16 + jnp.maximum(offset, 1)])

        else:
            arrived(blk, g_sem.at[16 + offset])
        for d in FAR4:
            sends.go(blk, blk, g_sem.at[34 + (d - 1) * 4 + p], xdev(d))
        sends.go(blk, blk, core_sem.at[p], core_dev)

    pass_on(0)

    @when(first & has_tile)
    def _():
        for d in NEAR4:
            arrived(ag_v.at[xi(-d), yc, :, 1, 0], g_sem.at[24 + d - 1])

    blk_y = ag_v.at[:, yc, :, 1, 0]
    for d in FAR8:
        sends.go(blk_y, blk_y, g_sem.at[46 + d - 1], ydev(d), first, has_tile)
    sends.go(blk_y, blk_y, core_sem.at[16], core_dev, first, has_tile)

    @when(odd & second)
    def _():
        for d in NEAR8:

            @when(yi(-d) < 7)
            def _():
                arrived(ag_v.at[:, jnp.minimum(yi(-d), 6), g, 1, 1], g_sem.at[27 + d - 1])

    blk_z = ag_v.at[:, :, g, 1, 1]
    for d in FAR8:
        sends.go(blk_z, blk_z, g_sem.at[53 + d - 1], zdev(d), odd, second)
    sends.go(blk_z, blk_z, core_sem.at[24], core_dev, odd, second)

    pass_on(1)
    pass_on(2)
    pass_on(3)

    for p in range(4):
        from_g = part(p)[1]
        for d in NEAR4:
            blk = ag_v.at[xi(-d), :, from_g, 0, c]
            arrived(blk, g_sem.at[34 + (d - 1) * 4 + p])
            sends.go(blk, blk, core_sem.at[4 + (d - 1) * 4 + p], core_dev)
    for d in NEAR8:
        cond = first & (yi(-d) < 7)
        blk = ag_v.at[:, jnp.minimum(yi(-d), 6), :, 1, 0]

        @when(cond)
        def _():
            arrived(blk, g_sem.at[46 + d - 1])

        sends.go(blk, blk, core_sem.at[16 + d], core_dev, cond)
        cond = second & (zi(-d) % 2 == 1)
        blk = ag_v.at[:, :, zi(-d) // 2, 1, 1]

        @when(cond)
        def _():
            arrived(blk, g_sem.at[53 + d - 1])

        sends.go(blk, blk, core_sem.at[24 + d], core_dev, cond)
    for p in range(4):
        from_g = part(p)[1]
        arrived(ag_v.at[a, :, from_g, 0, 1 - c], core_sem.at[p])
        for d in NEAR4:
            arrived(
                ag_v.at[xi(-d), :, from_g, 0, 1 - c], core_sem.at[4 + (d - 1) * 4 + p]
            )
    for d in (0,) + NEAR8:

        @when(second & (yi(-d) < 7))
        def _():
            arrived(ag_v.at[:, jnp.minimum(yi(-d), 6), :, 1, 0], core_sem.at[16 + d])

        @when(first & (zi(-d) % 2 == 1))
        def _():
            arrived(ag_v.at[:, :, zi(-d) // 2, 1, 1], core_sem.at[24 + d])

    loads[7].wait()
    loads[8].wait()
    loads[9].wait()
    pieces = [ag_v[i // 7, i % 7].reshape(256, 128) for i in range(28)]
    square = jnp.zeros((256, 128), F32)
    for i in range(28):
        item = pieces[i].astype(F32) / gain_v[i : i + 1, :]
        square = square + item * item
    inverse = lax.rsqrt(jnp.sum(square, axis=1, keepdims=True) * (1.0 / 3584) + 1e-6)
    both = jnp.dot(jnp.concatenate(pieces, axis=1), wgu_v[...], preferred_element_type=F32)
    both = both * inverse
    gate = both[:, 0:128]
    act = gate / (1.0 + jnp.exp(-gate)) * both[:, 128:256] * rw_v[...]
    act = jnp.concatenate(
        [
            act[grp * 64 + mb * 32 : grp * 64 + mb * 32 + 32]
            for mb in range(2)
            for grp in range(4)
        ],
        axis=0,
    ).astype(BF16)
    for n, d in enumerate((2, 1, 3, 0)):
        x = xi(d)
        down = jnp.dot(
            act,
            wd_v[:, pl.ds(pl.multiple_of(x * 896, 128), 896)],
            preferred_element_type=F32,
        )
        for mb in range(2):
            for k in range(7):
                unit_v[n % 2, :, mb * 7 + k, :] = down[
                    mb * 128 : (mb + 1) * 128, k * 128 : (k + 1) * 128
                ]
        pd_v[x] = unit_v[n % 2].astype(BF16).reshape(4, 2, 8, 2, 16, 128)
        sends.go(pd_v.at[x, :, :, :, 1 - c], r0_v.at[x], r_sem.at[d], core_dev)

    def target(p):
        offset = (4, 2, 6, 0)[p] + l * (-1, 3, -5, 7)[p]
        return offset, (z + offset) % 8 // 2

    for d in (2, 1, 3, 0):
        x = xi(d)
        arrived(r0_v.at[x], r_sem.at[d])
        qs_v[x] = (pd_v[x, :, :, :, c].astype(F32) + r0_v[x].astype(F32)).astype(BF16)
        if d > 0:
            for p in range(4):
                sends.go(
                    qs_v.at[x, target(p)[1], 0],
                    r1x_v.at[d - 1, p],
                    r_sem.at[4 + (d - 1) * 4 + p],
                    xdev(d),
                )
    for d in FAR8:
        sends.go(
            qs_v.at[:, :, 1, yi(d)], r1y_v.at[d - 1], r_sem.at[16 + d - 1], ydev(d), first
        )
    for d in FAR8:
        sends.go(
            qs_v.at[:, zi(d) // 2, 1],
            r1z_v.at[d - 1],
            r_sem.at[23 + d - 1],
            zdev(d),
            second,
            zi(d) % 2 == 1,
        )

    def total_of(own_block, ref, count):
        result = own_block.astype(F32)
        for i in range(count):
            result = result + ref[i].astype(F32)
        return result

    def all_arrived(ref, base, count):
        for i in range(count):
            arrived(ref.at[i], r_sem.at[base + i])

    for p in range(4):
        offset, to_g = target(p)
        result = qs_v[a, to_g, 0].astype(F32)
        for d in NEAR4:
            arrived(r1x_v.at[d - 1, p], r_sem.at[4 + (d - 1) * 4 + p])
            result = result + r1x_v[d - 1, p].astype(F32)
        s1x_v[p] = result.astype(BF16)
        device = {"grp": to_g, "exp": y * 2 + c}
        slot = jnp.maximum(offset - 1, 0)
        conds = (odd,) if p == 3 else ()
        sends.go(s1x_v.at[p], r2x_v.at[slot], r_sem.at[30 + slot], device, *conds)

    @when(first)
    def _():
        all_arrived(r1y_v, 16, 7)
        s1y_v[...] = total_of(qs_v[:, :, 1, y], r1y_v, 7).astype(BF16)

    for d in FAR4:
        sends.go(s1y_v.at[xi(d)], r2y_v.at[d - 1], r_sem.at[37 + d - 1], xdev(d), first)

    @when(second & odd)
    def _():
        all_arrived(r1z_v, 23, 7)
        s1z_v[...] = total_of(qs_v[:, g, 1], r1z_v, 7).astype(BF16)

    for d in FAR8:
        sends.go(
            s1z_v.at[:, yi(d)], r2z_v.at[d - 1], r_sem.at[40 + d - 1], ydev(d), second, odd
        )

    @when(first)
    def _():
        all_arrived(r2y_v, 37, 3)
        s2y_v[...] = total_of(s1y_v[a], r2y_v, 3).astype(BF16)

    for d in FAR8:
        sends.go(
            s2y_v.at[zi(d) // 2],
            r3_v.at[d - 1],
            r_sem.at[47 + d - 1],
            zdev(d),
            first,
            zi(d) % 2 == 1,
        )

    @when(even)
    def _():
        all_arrived(r2x_v, 30, 7)
        s2x_v[...] = total_of(s1x_v[3], r2x_v, 7).astype(BF16)

    for d in FAR8:
        sends.go(s2x_v.at[yi(d)], r3_v.at[d - 1], r_sem.at[47 + d - 1], ydev(d), even)

    @when(second & odd)
    def _():
        all_arrived(r2z_v, 40, 7)
        s2z_v[...] = total_of(s1z_v[:, y], r2z_v, 7).astype(BF16)

    for d in FAR4:
        sends.go(s2z_v.at[xi(d)], r3_v.at[d - 1], r_sem.at[47 + d - 1], xdev(d), second, odd)

    pltpu.make_async_copy(o_v, o_v, big_sem.at[2]).wait()
    sends.drain()

    @when(has_tile)
    def _():
        lax.fori_loop(0, 16, hidden_done, 0)

    @when(even)
    def _():
        all_arrived(r3_v, 47, 7)
        fin_v[...] = total_of(s2x_v[y], r3_v, 7)

    @when(odd & first)
    def _():
        all_arrived(r3_v, 47, 7)
        fin_v[...] = total_of(s2y_v[g], r3_v, 7)

    @when(odd & second)
    def _():
        all_arrived(r3_v, 47, 3)
        fin_v[...] = total_of(s2z_v[a], r3_v, 3)

    rows = [
        jnp.concatenate(
            [fin_v[mb * 7 + k : mb * 7 + k + 1, :] + o_v[mb, k] for k in range(7)], axis=1
        )
        for mb in range(2)
    ]
    out_ref[...] = jnp.concatenate(rows, axis=0).astype(BF16)


def body(
    resid,
    queries,
    cache,
    lengths,
    w_value,
    w_out,
    norm_gain,
    route_ids,
    route_weights,
    w_gate,
    w_up,
    w_down,
):
    hbm = pl.BlockSpec(memory_space=pl.ANY)
    vmem = pl.BlockSpec(memory_space=pltpu.VMEM)
    smem = pl.BlockSpec(memory_space=pltpu.SMEM)

    def bf(*shape):
        return pltpu.VMEM(shape, BF16)

    def f32(*shape):
        return pltpu.VMEM(shape, F32)

    def dma(count):
        return pltpu.SemaphoreType.DMA((count,))

    return pl.pallas_call(
        kernel,
        out_shape=jax.ShapeDtypeStruct((2, 896), BF16),
        in_specs=[smem, vmem] + [hbm] * 10,
        out_specs=vmem,
        scratch_shapes=[
            bf(2, 64, 576),
            bf(2, 576, 512),
            bf(16, 128),
            pltpu.VMEM((2, 8, 128), jnp.int32),
            f32(2, 8, 128),
            bf(4, 2, 32, 512),
            bf(4, 2, 32, 896),
            bf(3584, 256),
            bf(128, 3584),
            f32(256, 128),
            f32(28, 128),
            bf(4, 2, 16, 640),
            bf(3, 2, 16, 640),
            f32(16, 8, 128),
            bf(8, 16, 128),
            bf(32, 16, 128),
            f32(32, 16, 128),
            bf(7, 4, 16, 128),
            bf(32, 16, 128),
            f32(16, 128),
            bf(4, 7, 4, 2, 2, 16, 128),
            bf(4, 4, 2, 8, 2, 16, 128),
            bf(4, 4, 2, 8, 16, 128),
            bf(4, 4, 2, 8, 16, 128),
            bf(3, 4, 8, 16, 128),
            bf(7, 4, 4, 16, 128),
            bf(7, 4, 8, 16, 128),
            bf(4, 8, 16, 128),
            bf(4, 4, 16, 128),
            bf(4, 8, 16, 128),
            bf(7, 8, 16, 128),
            bf(3, 4, 16, 128),
            bf(7, 4, 16, 128),
            bf(8, 16, 128),
            bf(4, 16, 128),
            bf(4, 16, 128),
            bf(7, 16, 128),
            f32(16, 1, 128),
            f32(2, 7, 1, 128),
            f32(2, 128, 16, 128),
            f32(16, 128),
            dma(10),
            dma(SEND_SEMS),
            dma(16),
            dma(6),
            dma(3),
            dma(3),
            dma(60),
            dma(32),
            dma(54),
        ],
        compiler_params=pltpu.CompilerParams(
            collective_id=0, has_side_effects=True, vmem_limit_bytes=56 * 1024 * 1024
        ),
        name="layer",
    )(
        lengths.reshape(1, 2),
        norm_gain.reshape(28, 128),
        queries[:, 0],
        jnp.swapaxes(cache[:, 0], 1, 2),
        resid,
        jnp.swapaxes(route_ids, 1, 2),
        jnp.swapaxes(route_weights, 1, 2),
        jnp.swapaxes(w_value, 1, 2),
        w_out,
        w_gate[0],
        w_up[0],
        w_down[0],
    ).reshape(2, 1, 896)


def solution(mesh):
    return jax.shard_map(
        body,
        mesh=mesh,
        in_specs=(
            P(None, "grp", None),
            P(None, ("grp", "exp"), None, None),
            P(None, ("grp", "exp"), "attn", None),
            P(None, ("grp", "exp")),
            P("exp", None, "attn"),
            P("exp", "attn", None),
            P(),
            P(),
            P(),
            P("exp", None, ("attn", "grp")),
            P("exp", None, ("attn", "grp")),
            P("exp", ("attn", "grp"), None),
        ),
        out_specs=P(None, ("grp", "exp"), "attn"),
        check_vma=False,
    )
```

```python
import jax
import jax.numpy as jnp
from jax import lax
from jax.experimental import pallas as pl
from jax.experimental.pallas import tpu as pltpu
from jax.sharding import PartitionSpec as P

MESH = pl.DeviceIdType.MESH
F32 = jnp.float32
BF16 = jnp.bfloat16
SCALE = (128 + 64) ** -0.5
NT = (((1,), (1,)), ((), ()))


def remote(src, dst, send_sem, recv_sem, device):
    return pltpu.make_async_remote_copy(
        src_ref=src,
        dst_ref=dst,
        send_sem=send_sem,
        recv_sem=recv_sem,
        device_id=device,
        device_id_type=MESH,
    )


class Sends:
    def __init__(self, sems):
        self.sems = sems
        self.used = 0
        self.pending = []

    def go(self, src, dst, recv_sem, device, *conds):
        copy = remote(src, dst, self.sems.at[self.used], recv_sem, device)
        self.used += 1
        cond = None
        for item in conds:
            cond = item if cond is None else cond & item
        if cond is None:
            copy.start()
        else:
            pl.when(cond)(copy.start)
        self.pending.append((cond, copy))

    def drain(self):
        for cond, copy in self.pending:
            if cond is None:
                copy.wait_send()
            else:
                pl.when(cond)(copy.wait_send)
        self.pending = []


FAR8 = (4, 3, 5, 2, 6, 1, 7)
FAR4 = (2, 1, 3)
NEAR8 = (1, 7, 2, 6, 3, 5, 4)
NEAR4 = (1, 3, 2)
SEND_SEMS = 232


def kernel(
    len_hbm,
    gain_hbm,
    q_hbm,
    cache_hbm,
    resid_hbm,
    ids_hbm,
    wts_hbm,
    wv_hbm,
    wo_hbm,
    wg_hbm,
    wu_hbm,
    wd_hbm,
    out_ref,
    len_v,
    gain16_v,
    q_v,
    cache_v,
    res_v,
    ids_v,
    wts_v,
    wvt_v,
    wo_v,
    wgu_v,
    wd_v,
    rw_v,
    gain_v,
    s1_v,
    p1_v,
    c32_v,
    s2_v,
    p2_v,
    c2_v,
    s3_v,
    p3_v,
    hid_v,
    ag_v,
    qs_v,
    r1x_v,
    r1y_v,
    r1z_v,
    s1x_v,
    s1y_v,
    s1z_v,
    r2x_v,
    r2y_v,
    r2z_v,
    s2x_v,
    s2y_v,
    s2z_v,
    r3_v,
    f_v,
    o_v,
    unit_v,
    fin_v,
    lsem,
    send_sems,
    loop_sems,
    wsem,
    p1_sem,
    big_sem,
    g_sem,
    core_sem,
    r_sem,
):
    a = lax.axis_index("attn")
    g = lax.axis_index("grp")
    e = lax.axis_index("exp")
    c = e % 2
    y = (e // 2) % 8
    l = e // 16
    z = 2 * g + l
    yc = jnp.minimum(y, 6)
    has_tile = y < 7
    even = l == 0
    odd = l == 1
    first = c == 0
    second = c == 1
    sends = Sends(send_sems)
    when = pl.when

    def xi(d):
        return (a + d + 4) % 4

    def yi(d):
        return (y + d + 8) % 8

    def zi(d):
        return (z + d + 8) % 8

    def xdev(d):
        return {"attn": xi(d)}

    def ydev(d):
        return {"exp": l * 16 + yi(d) * 2 + c}

    def zdev(d):
        return {"grp": zi(d) // 2, "exp": (zi(d) % 2) * 16 + y * 2 + c}

    core_dev = {"exp": e + 1 - 2 * c}

    def arrived(dst, sem):
        remote(dst, dst, send_sems.at[0], sem, core_dev).wait_recv()

    chunk = pl.multiple_of((a * 7 + yc) * 128, 128)
    loads = [
        pltpu.make_async_copy(src, dst, lsem.at[i])
        for i, (src, dst) in enumerate(
            [
                (q_hbm, q_v),
                (cache_hbm, cache_v),
                (wv_hbm, wvt_v.at[a]),
                (
                    resid_hbm.at[l, pl.ds(pl.multiple_of(c * 16, 16), 16), pl.ds(chunk, 128)],
                    res_v,
                ),
                (ids_hbm, ids_v),
                (wts_hbm, wts_v),
                (
                    wo_hbm.at[:, :, pl.ds(pl.multiple_of(a * 896, 128), 896)],
                    wo_v.at[a],
                ),
                (wg_hbm, wgu_v.at[c, :, pl.ds(0, 128)]),
                (wu_hbm, wgu_v.at[c, :, pl.ds(128, 128)]),
                (wd_hbm, wd_v.at[c]),
                (len_hbm, len_v),
                (gain_hbm, gain16_v),
            ]
        )
    ]
    for i in (1, 0, 10):
        loads[i].start()

    barrier = pltpu.get_barrier_semaphore()

    def greet(device):
        pl.semaphore_signal(barrier, inc=1, device_id=device, device_id_type=MESH)


    def greet_plane(i, carry):
        greet({"exp": (e + i) % 32})
        return carry

    lax.fori_loop(8, 32, greet_plane, 0)
    for d in FAR8:
        greet(zdev(d))
    for d in FAR4:
        greet(xdev(d))
    lax.fori_loop(1, 8, greet_plane, 0)

    for i in (11, 2, 3, 4, 5, 6, 7, 8, 9):
        loads[i].start()
    loads[11].wait()
    gain_v[...] = gain16_v[...].astype(F32)
    unit_v[:, :, 8:16, :] = jnp.zeros((2, 64, 8, 128), F32)

    loads[10].wait()
    loads[0].wait()
    loads[1].wait()
    row = lax.broadcasted_iota(jnp.int32, (64, 64), 0)
    col = lax.broadcasted_iota(jnp.int32, (64, 64), 1)
    head = ((row & 15) >> 1) * 8 + (row >> 4) * 2 + (row & 1)
    perm = jnp.where(head == col, 1.0, 0.0).astype(BF16)
    pos = a * 512 + lax.broadcasted_iota(jnp.int32, (64, 512), 1)
    lane = lax.broadcasted_iota(jnp.int32, (64, 128), 1)
    for mb in range(2):
        qp = jnp.dot(perm, q_v[mb], preferred_element_type=F32).astype(BF16)
        scores = jnp.dot(qp, cache_v[mb], preferred_element_type=F32) * SCALE
        visible = pos < len_v[0, mb]
        top = jnp.max(jnp.where(visible, scores, -1e30), axis=1, keepdims=True)
        top = top.astype(BF16).astype(F32)
        weights = jnp.where(visible, jnp.exp(scores - top), 0.0)
        total = jnp.sum(weights, axis=1, keepdims=True)
        acc = lax.dot_general(
            weights.astype(BF16), cache_v[mb, 0:512, :], NT, preferred_element_type=F32
        )
        hi = total.astype(BF16).astype(F32)
        stats = jnp.where(lane == 0, top, jnp.where(lane == 1, hi, total - hi))
        s1_v[:, mb, :, 0:512] = acc.astype(BF16).reshape(4, 16, 512)
        s1_v[:, mb, :, 512:640] = stats.astype(BF16).reshape(4, 16, 128)
    pl.semaphore_wait(barrier, 41)
    for d in FAR4:
        sends.go(s1_v.at[xi(d)], p1_v.at[d - 1], p1_sem.at[d - 1], xdev(d))

    loads[4].wait()
    loads[5].wait()
    for mb in range(2):
        for s in range(2):
            gate = jnp.sum(
                jnp.where(ids_v[mb] == e - c + s, wts_v[mb], 0.0), axis=0, keepdims=True
            )
            gate = jnp.broadcast_to(gate, (128, 128)).T
            for grp in range(4):
                at = grp * 32
                rw_v[s, mb * 64 + grp * 16 : mb * 64 + grp * 16 + 16, :] = jnp.where(
                    first, gate[at : at + 16, :], gate[at + 16 : at + 32, :]
                )

    loads[2].wait()
    for d in FAR4:
        sends.go(wvt_v.at[a], wvt_v.at[a], wsem.at[d - 1], xdev(d))

    for d in range(1, 4):
        arrived(p1_v.at[d - 1], p1_sem.at[d - 1])
    blocks = [s1_v[a]] + [p1_v[d] for d in range(3)]
    blocks = [b.astype(F32).reshape(32, 640) for b in blocks]
    tops = [b[:, 512:513] for b in blocks]
    row_top = jnp.maximum(jnp.maximum(tops[0], tops[1]), jnp.maximum(tops[2], tops[3]))
    ctx_sum = jnp.zeros((32, 512), F32)
    row_total = jnp.zeros((32, 1), F32)
    for b, t in zip(blocks, tops):
        factor = jnp.exp(t - row_top)
        ctx_sum = ctx_sum + b[:, 0:512] * factor
        row_total = row_total + (b[:, 513:514] + b[:, 514:515]) * factor
    context = ctx_sum / row_total
    for mb in range(2):
        for k in range(4):
            c32_v[:, mb * 4 + k, :] = context[
                mb * 16 : (mb + 1) * 16, k * 128 : (k + 1) * 128
            ]
    s2_v[...] = c32_v[...].reshape(8, 16, 128).astype(BF16)

    for s_off in (2, 1, 3, 0):
        for d in FAR4 + (0,):
            for half in (1, 0):
                j = (half + l) % 2 * 4 + (y // 2 + s_off) % 4
                to_e = 4 * j + a
                device = {"attn": xi(d), "exp": to_e}
                if s_off == 0 and d == 0:
                    mine = to_e == e
                    near = pltpu.make_async_copy(s2_v.at[j], p2_v.at[e], big_sem.at[0])
                    when(mine)(near.start)
                    sends.go(
                        s2_v.at[j], p2_v.at[e], big_sem.at[0], device, jnp.logical_not(mine)
                    )
                else:
                    sends.go(s2_v.at[j], p2_v.at[e], big_sem.at[0], device)

    for d in FAR4:
        sends.go(
            wo_hbm.at[:, :, pl.ds(pl.multiple_of(xi(d) * 896, 128), 896)],
            wo_v.at[a],
            wsem.at[2 + d],
            xdev(d),
        )
    loads[6].wait()
    for d in range(1, 4):
        arrived(wvt_v.at[xi(-d)], wsem.at[d - 1])
        arrived(wo_v.at[xi(-d)], wsem.at[2 + d])
    pltpu.make_async_copy(p2_v, p2_v, big_sem.at[0]).wait()
    c2_v[...] = p2_v[...].astype(F32)
    out = jnp.zeros((64, 896), F32)
    for h in range(2):
        rows = [
            jnp.concatenate([c2_v[:, h * 8 + mb * 4 + k, :] for k in range(4)], axis=1)
            for mb in range(2)
        ]
        ctx = jnp.concatenate(rows, axis=0).astype(BF16)
        values = lax.dot_general(
            ctx, wvt_v[:, h].reshape(128, 512), NT, preferred_element_type=F32
        ).astype(BF16)
        out = out + jnp.dot(
            values, wo_v[:, h].reshape(128, 896), preferred_element_type=F32
        )
    for k in range(7):
        s3_v[k] = out[:, k * 128 : (k + 1) * 128].astype(BF16).reshape(4, 16, 128)

    for d in FAR8 + (0,):
        for half in (1, 0):
            for core in (1, 0):
                if d == 0 and half == 0 and core == 0:
                    continue
                to_l, to_c = (l + half) % 2, (c + core) % 2
                src = s3_v.at[jnp.minimum(yi(d), 6), to_l * 2 + to_c]
                device = {"exp": to_l * 16 + yi(d) * 2 + to_c}
                sends.go(src, p3_v.at[e], big_sem.at[1], device, yi(d) < 7)

    halves = [
        (wg_hbm, wgu_v.at[c, :, pl.ds(0, 128)], wgu_v.at[1 - c, :, pl.ds(0, 128)]),
        (wu_hbm, wgu_v.at[c, :, pl.ds(128, 128)], wgu_v.at[1 - c, :, pl.ds(128, 128)]),
        (wd_hbm, wd_v.at[c], wd_v.at[1 - c]),
    ]
    for i, (src, dst, _) in enumerate(halves):
        sends.go(src, dst, core_sem.at[i], core_dev)

    @when(has_tile)
    def _():
        pltpu.make_async_copy(s3_v.at[yc, l * 2 + c], p3_v.at[e], big_sem.at[1]).start()
        loads[3].wait()
        pltpu.make_async_copy(p3_v, p3_v, big_sem.at[1]).wait()
        attended = jnp.sum(p3_v[...].astype(F32), axis=0)
        hidden = res_v[...].astype(F32) + attended
        hid_v[...] = hidden
        ag_v[a, yc, l, g] = (hidden * gain_v[pl.ds(a * 7 + yc, 1), :]).astype(BF16)

    @when(jnp.logical_not(has_tile))
    def _():
        loads[3].wait()

    own = ag_v.at[a, yc, l, g]
    for d in FAR8:
        sends.go(own, own, g_sem.at[d - 1], ydev(d), even, has_tile)
    for d in FAR8:
        sends.go(own, own, g_sem.at[7 + d - 1], zdev(d), odd, first, has_tile)
    for d in FAR4:
        sends.go(own, own, g_sem.at[14 + d - 1], xdev(d), odd, second, has_tile)

    def hidden_copy(i):
        to_e = c * 16 + i
        far = remote(
            f_v.at[i], o_v.at[l, yc], loop_sems.at[i], big_sem.at[2], {"exp": to_e}
        )
        return to_e == e, far

    def hidden_go(i, carry):
        mine, far = hidden_copy(i)

        @when(mine)
        def _():
            pltpu.make_async_copy(f_v.at[i], o_v.at[l, yc], big_sem.at[2]).start()

        pl.when(jnp.logical_not(mine))(far.start)
        return carry

    def hidden_done(i, carry):
        mine, far = hidden_copy(i)
        pl.when(jnp.logical_not(mine))(far.wait_send)
        return carry

    @when(has_tile)
    def _():
        for i in range(16):
            f_v[i] = hid_v[i : i + 1, :]
        lax.fori_loop(0, 16, hidden_go, 0)

    @when(odd & second & has_tile)
    def _():
        for d in NEAR4:
            arrived(ag_v.at[xi(-d), yc, 1, g], g_sem.at[14 + d - 1])

    for d in FAR8:
        blk = ag_v.at[:, yc, 1, g]
        sends.go(blk, blk, g_sem.at[27 + d - 1], ydev(d), odd, second, has_tile)

    @when(even)
    def _():
        for d in NEAR8:

            @when(yi(-d) < 7)
            def _():
                arrived(ag_v.at[a, jnp.minimum(yi(-d), 6), 0, g], g_sem.at[d - 1])

    for d in FAR8:
        blk = ag_v.at[a, :, 0, g]
        sends.go(blk, blk, g_sem.at[17 + d - 1], zdev(d), even)

    @when(first & has_tile)
    def _():
        for d in NEAR8:

            @when(zi(-d) % 2 == 1)
            def _():
                arrived(ag_v.at[a, yc, 1, zi(-d) // 2], g_sem.at[7 + d - 1])

    for d in FAR4:
        blk = ag_v.at[a, yc, 1]
        sends.go(blk, blk, g_sem.at[24 + d - 1], xdev(d), first, has_tile)

    def part(p):
        offset = (0, 2, 6, 4)[p] + l * (1, 5, -3, 1)[p]
        return offset, (z - offset + 8) % 8 // 2

    def pass_on(p):
        offset, from_g = part(p)
        blk = ag_v.at[a, :, 0, from_g]
        if p == 0:

            @when(odd)
            def _():
                arrived(blk, g_sem.at[16 + jnp.maximum(offset, 1)])

        else:
            arrived(blk, g_sem.at[16 + offset])
        for d in FAR4:
            sends.go(blk, blk, g_sem.at[34 + (d - 1) * 4 + p], xdev(d))

    pass_on(0)

    @when(first & has_tile)
    def _():
        for d in NEAR4:
            arrived(ag_v.at[xi(-d), yc, 1], g_sem.at[24 + d - 1])

    blk_y = ag_v.at[:, yc, 1]
    for d in FAR8:
        sends.go(blk_y, blk_y, g_sem.at[46 + d - 1], ydev(d), first, has_tile)

    @when(odd & second)
    def _():
        for d in NEAR8:

            @when(yi(-d) < 7)
            def _():
                arrived(ag_v.at[:, jnp.minimum(yi(-d), 6), 1, g], g_sem.at[27 + d - 1])

    blk_z = ag_v.at[:, :, 1, g]
    for d in FAR8:
        sends.go(blk_z, blk_z, g_sem.at[53 + d - 1], zdev(d), odd, second)

    pass_on(1)
    pass_on(2)
    pass_on(3)

    for p in range(4):
        from_g = part(p)[1]
        for d in NEAR4:
            arrived(ag_v.at[xi(-d), :, 0, from_g], g_sem.at[34 + (d - 1) * 4 + p])
    for d in NEAR8:

        @when(first & (yi(-d) < 7))
        def _():
            arrived(ag_v.at[:, jnp.minimum(yi(-d), 6), 1], g_sem.at[46 + d - 1])

        @when(second & (zi(-d) % 2 == 1))
        def _():
            arrived(ag_v.at[:, :, 1, zi(-d) // 2], g_sem.at[53 + d - 1])

    loads[7].wait()
    loads[8].wait()
    loads[9].wait()
    for i, (_, _, dst) in enumerate(halves):
        arrived(dst, core_sem.at[i])
    pieces = [ag_v[i // 7, i % 7].reshape(128, 128) for i in range(28)]
    square = jnp.zeros((128, 128), F32)
    for i in range(28):
        item = pieces[i].astype(F32) / gain_v[i : i + 1, :]
        square = square + item * item
    inverse = lax.rsqrt(jnp.sum(square, axis=1, keepdims=True) * (1.0 / 3584) + 1e-6)
    rows = jnp.concatenate(pieces, axis=1)
    acts = []
    for s in range(2):
        both = jnp.dot(rows, wgu_v[s], preferred_element_type=F32) * inverse
        gate = both[:, 0:128]
        acts.append(gate / (1.0 + jnp.exp(-gate)) * both[:, 128:256] * rw_v[s])
    act = jnp.concatenate(acts, axis=1).astype(BF16)
    def target(p):
        offset = (4, 2, 6, 0)[p] + (l + c) % 2 * (-1, 3, -5, 7)[p]
        return offset, (z + offset) % 8 // 2

    for n, d in enumerate((2, 1, 3, 0)):
        x = xi(d)
        down = jnp.dot(
            act,
            wd_v[:, :, pl.ds(pl.multiple_of(x * 896, 128), 896)].reshape(256, 896),
            preferred_element_type=F32,
        )
        for mb in range(2):
            for k in range(7):
                unit_v[n % 2, :, mb * 7 + k, :] = down[
                    mb * 64 : (mb + 1) * 64, k * 128 : (k + 1) * 128
                ]
        qs_v[x] = unit_v[n % 2].astype(BF16).reshape(4, 8, 2, 16, 128)
        if d > 0:
            for p in range(4):
                sends.go(
                    qs_v.at[x, target(p)[1], :, 0],
                    r1x_v.at[d - 1, p],
                    r_sem.at[(d - 1) * 4 + p],
                    xdev(d),
                )

    for d in FAR8:
        sends.go(
            qs_v.at[:, :, yi(d), 1], r1y_v.at[d - 1], r_sem.at[12 + d - 1], ydev(d), first
        )
    for d in FAR8:
        sends.go(
            qs_v.at[:, zi(d) // 2, :, 1],
            r1z_v.at[d - 1],
            r_sem.at[19 + d - 1],
            zdev(d),
            second,
            zi(d) % 2 == 1,
        )

    def total_of(blocks):
        result = blocks[0].astype(F32)
        for blk in blocks[1:]:
            result = result + blk.astype(F32)
        return result

    def take(ref, base, items):
        for i in items:
            arrived(ref.at[i], r_sem.at[base + i])
        return [ref[i] for i in items]

    for p in range(4):
        offset, to_g = target(p)
        result = qs_v[a, to_g, :, 0].astype(F32)
        for d in NEAR4:
            arrived(r1x_v.at[d - 1, p], r_sem.at[(d - 1) * 4 + p])
            result = result + r1x_v[d - 1, p].astype(F32)
        s1x_v[p] = result.astype(BF16)
        device = {"grp": to_g, "exp": c * 16 + y * 2 + c}
        slot = jnp.maximum(offset - 1, 0)
        conds = (l != c,) if p == 3 else ()
        sends.go(s1x_v.at[p], r2x_v.at[slot], r_sem.at[26 + slot], device, *conds)

    @when(first)
    def _():
        s1y_v[...] = total_of([qs_v[:, :, y, 1]] + take(r1y_v, 12, range(7))).astype(BF16)

    for d in FAR4:
        sends.go(s1y_v.at[xi(d)], r2y_v.at[d - 1], r_sem.at[33 + d - 1], xdev(d), first)

    @when(second & odd)
    def _():
        s1z_v[...] = total_of([qs_v[:, g, :, 1]] + take(r1z_v, 19, range(7))).astype(BF16)

    for d in FAR8:
        sends.go(
            s1z_v.at[:, yi(d)], r2z_v.at[d - 1], r_sem.at[36 + d - 1], ydev(d), second, odd
        )

    @when(first)
    def _():
        s2y_v[...] = total_of([s1y_v[a]] + take(r2y_v, 33, range(3))).astype(BF16)

    for d in FAR8 + (0,):
        device = {"grp": zi(d) // 2, "exp": y * 2 + 1}
        sends.go(
            s2y_v.at[zi(d) // 2], r3_v.at[d], r_sem.at[43 + d], device, first, zi(d) % 2 == 0
        )

    @when(l == c)
    def _():
        s2x_v[...] = total_of([s1x_v[3]] + take(r2x_v, 26, range(7))).astype(BF16)

    for d in FAR8 + (0,):
        device = {"exp": l * 16 + yi(d) * 2}
        conds = (l == c, second) if d == 0 else (l == c,)
        sends.go(s2x_v.at[yi(d)], r3_v.at[d], r_sem.at[43 + d], device, *conds)

    @when(second & odd)
    def _():
        s2z_v[...] = total_of([s1z_v[:, y]] + take(r2z_v, 36, range(7))).astype(BF16)

    for d in FAR4:
        sends.go(s2z_v.at[xi(d)], r3_v.at[d], r_sem.at[43 + d], xdev(d), second, odd)

    pltpu.make_async_copy(o_v, o_v, big_sem.at[2]).wait()
    sends.drain()

    @when(has_tile)
    def _():
        lax.fori_loop(0, 16, hidden_done, 0)

    @when(even & first)
    def _():
        fin_v[...] = total_of([s2x_v[y]] + take(r3_v, 43, range(1, 8)))

    @when(l != c)
    def _():
        fin_v[...] = total_of(take(r3_v, 43, range(8)))

    @when(odd & second)
    def _():
        fin_v[...] = total_of([s2z_v[a]] + take(r3_v, 43, range(1, 4)))

    rows = [
        jnp.concatenate(
            [fin_v[mb * 7 + k : mb * 7 + k + 1, :] + o_v[mb, k] for k in range(7)], axis=1
        )
        for mb in range(2)
    ]
    out_ref[...] = jnp.concatenate(rows, axis=0).astype(BF16)


def body(
    resid,
    queries,
    cache,
    lengths,
    w_value,
    w_out,
    norm_gain,
    route_ids,
    route_weights,
    w_gate,
    w_up,
    w_down,
):
    hbm = pl.BlockSpec(memory_space=pl.ANY)
    vmem = pl.BlockSpec(memory_space=pltpu.VMEM)

    def bf(*shape):
        return pltpu.VMEM(shape, BF16)

    def f32(*shape):
        return pltpu.VMEM(shape, F32)

    def dma(count):
        return pltpu.SemaphoreType.DMA((count,))

    return pl.pallas_call(
        kernel,
        out_shape=jax.ShapeDtypeStruct((2, 896), BF16),
        in_specs=[hbm] * 12,
        out_specs=vmem,
        scratch_shapes=[
            pltpu.SMEM((1, 2), jnp.int32),
            bf(28, 128),
            bf(2, 64, 576),
            bf(2, 576, 512),
            bf(16, 128),
            pltpu.VMEM((2, 8, 128), jnp.int32),
            f32(2, 8, 128),
            bf(4, 2, 32, 512),
            bf(4, 2, 32, 896),
            bf(2, 3584, 256),
            bf(2, 128, 3584),
            f32(2, 128, 128),
            f32(28, 128),
            bf(4, 2, 16, 640),
            bf(3, 2, 16, 640),
            f32(16, 8, 128),
            bf(8, 16, 128),
            bf(32, 16, 128),
            f32(32, 16, 128),
            bf(7, 4, 16, 128),
            bf(32, 16, 128),
            f32(16, 128),
            bf(4, 7, 2, 4, 16, 128),
            bf(4, 4, 8, 2, 16, 128),
            bf(3, 4, 8, 16, 128),
            bf(7, 4, 4, 16, 128),
            bf(7, 4, 8, 16, 128),
            bf(4, 8, 16, 128),
            bf(4, 4, 16, 128),
            bf(4, 8, 16, 128),
            bf(7, 8, 16, 128),
            bf(3, 4, 16, 128),
            bf(7, 4, 16, 128),
            bf(8, 16, 128),
            bf(4, 16, 128),
            bf(4, 16, 128),
            bf(8, 16, 128),
            f32(16, 1, 128),
            f32(2, 7, 1, 128),
            f32(2, 64, 16, 128),
            f32(16, 128),
            dma(12),
            dma(SEND_SEMS),
            dma(16),
            dma(6),
            dma(3),
            dma(3),
            dma(60),
            dma(3),
            dma(51),
        ],
        compiler_params=pltpu.CompilerParams(
            collective_id=0, has_side_effects=True, vmem_limit_bytes=56 * 1024 * 1024
        ),
        name="layer",
    )(
        lengths.reshape(1, 2),
        norm_gain.reshape(28, 128),
        queries[:, 0],
        jnp.swapaxes(cache[:, 0], 1, 2),
        resid,
        jnp.swapaxes(route_ids, 1, 2),
        jnp.swapaxes(route_weights, 1, 2),
        jnp.swapaxes(w_value, 1, 2),
        w_out,
        w_gate[0],
        w_up[0],
        w_down[0],
    ).reshape(2, 1, 896)


def solution(mesh):
    return jax.shard_map(
        body,
        mesh=mesh,
        in_specs=(
            P(None, "grp", None),
            P(None, ("grp", "exp"), None, None),
            P(None, ("grp", "exp"), "attn", None),
            P(None, ("grp", "exp")),
            P("exp", None, "attn"),
            P("exp", "attn", None),
            P(),
            P(),
            P(),
            P("exp", None, ("attn", "grp")),
            P("exp", None, ("attn", "grp")),
            P("exp", ("attn", "grp"), None),
        ),
        out_specs=P(None, ("grp", "exp"), "attn"),
        check_vma=False,
    )
```

```python
import jax
import jax.numpy as jnp
from jax import lax
from jax.experimental import pallas as pl
from jax.experimental.pallas import tpu as pltpu
from jax.sharding import PartitionSpec as P

MESH = pl.DeviceIdType.MESH
F32 = jnp.float32
BF16 = jnp.bfloat16
SCALE = (128 + 64) ** -0.5
NT = (((1,), (1,)), ((), ()))


def remote(src, dst, send_sem, recv_sem, device):
    return pltpu.make_async_remote_copy(
        src_ref=src,
        dst_ref=dst,
        send_sem=send_sem,
        recv_sem=recv_sem,
        device_id=device,
        device_id_type=MESH,
    )


class Sends:
    def __init__(self, sems):
        self.sems = sems
        self.used = 0
        self.pending = []

    def go(self, src, dst, recv_sem, device, *conds):
        copy = remote(src, dst, self.sems.at[self.used], recv_sem, device)
        self.used += 1
        cond = None
        for item in conds:
            cond = item if cond is None else cond & item
        if cond is None:
            copy.start()
        else:
            pl.when(cond)(copy.start)
        self.pending.append((cond, copy))

    def drain(self):
        for cond, copy in self.pending:
            if cond is None:
                copy.wait_send()
            else:
                pl.when(cond)(copy.wait_send)
        self.pending = []


FAR8 = (4, 3, 5, 2, 6, 1, 7)
FAR4 = (2, 1, 3)
QUARTERS = (2, 1, 3, 0)
NEAR8 = (1, 7, 2, 6, 3, 5, 4)
NEAR4 = (1, 3, 2)
SEND_SEMS = 290


def kernel(
    len_hbm,
    gain_hbm,
    q_hbm,
    cache_hbm,
    resid_hbm,
    ids_hbm,
    wts_hbm,
    wv_hbm,
    wo_hbm,
    wg_hbm,
    wu_hbm,
    wd_hbm,
    out_ref,
    len_v,
    gain16_v,
    q_v,
    cache_v,
    res_v,
    ids_v,
    wts_v,
    wvt_v,
    wo_v,
    wgu_v,
    wd_v,
    rw_v,
    gain_v,
    s1_v,
    p1_v,
    c32_v,
    s2_v,
    p2_v,
    c2_v,
    s3_v,
    p3_v,
    hid_v,
    ag_v,
    qs_v,
    r1x_v,
    r1y_v,
    r1z_v,
    s1x_v,
    s1y_v,
    s1z_v,
    r2x_v,
    r2y_v,
    r2z_v,
    s2x_v,
    s2y_v,
    s2z_v,
    r3_v,
    f_v,
    o_v,
    unit_v,
    fin_v,
    lsem,
    send_sems,
    loop_sems,
    wsem,
    p1_sem,
    big_sem,
    g_sem,
    core_sem,
    r_sem,
):
    a = lax.axis_index("attn")
    g = lax.axis_index("grp")
    e = lax.axis_index("exp")
    c = e % 2
    y = (e // 2) % 8
    l = e // 16
    z = 2 * g + l
    yc = jnp.minimum(y, 6)
    has_tile = y < 7
    even = l == 0
    odd = l == 1
    first = c == 0
    second = c == 1
    sends = Sends(send_sems)
    when = pl.when

    def xi(d):
        return (a + d + 4) % 4

    def yi(d):
        return (y + d + 8) % 8

    def zi(d):
        return (z + d + 8) % 8

    def xdev(d):
        return {"attn": xi(d)}

    def ydev(d):
        return {"exp": l * 16 + yi(d) * 2 + c}

    def zdev(d):
        return {"grp": zi(d) // 2, "exp": (zi(d) % 2) * 16 + y * 2 + c}

    core_dev = {"exp": e + 1 - 2 * c}

    def arrived(dst, sem):
        remote(dst, dst, send_sems.at[0], sem, core_dev).wait_recv()

    chunk = pl.multiple_of((a * 7 + yc) * 128, 128)
    loads = [
        pltpu.make_async_copy(src, dst, lsem.at[i])
        for i, (src, dst) in enumerate(
            [
                (q_hbm, q_v),
                (cache_hbm, cache_v),
                (wv_hbm, wvt_v.at[a]),
                (
                    resid_hbm.at[l, pl.ds(pl.multiple_of(c * 16, 16), 16), pl.ds(chunk, 128)],
                    res_v,
                ),
                (ids_hbm, ids_v),
                (wts_hbm, wts_v),
                (
                    wo_hbm.at[:, :, pl.ds(pl.multiple_of(a * 896, 128), 896)],
                    wo_v.at[a],
                ),
                (wg_hbm, wgu_v.at[c, :, pl.ds(0, 128)]),
                (wu_hbm, wgu_v.at[c, :, pl.ds(128, 128)]),
                (wd_hbm, wd_v.at[c]),
                (len_hbm, len_v),
                (gain_hbm, gain16_v),
            ]
        )
    ]
    for i in (1, 0, 10):
        loads[i].start()

    barrier = pltpu.get_barrier_semaphore()

    def greet(device):
        pl.semaphore_signal(barrier, inc=1, device_id=device, device_id_type=MESH)


    def greet_plane(i, carry):
        greet({"exp": (e + i) % 32})
        return carry

    lax.fori_loop(8, 32, greet_plane, 0)
    for d in FAR8:
        greet(zdev(d))
    for d in FAR4:
        greet(xdev(d))
    lax.fori_loop(1, 8, greet_plane, 0)

    for i in (11, 2, 3, 4, 5, 6, 7, 8, 9):
        loads[i].start()
    loads[11].wait()
    gain_v[...] = gain16_v[...].astype(F32)
    unit_v[:, :, 8:16, :] = jnp.zeros((2, 64, 8, 128), F32)

    loads[10].wait()
    loads[0].wait()
    loads[1].wait()
    row = lax.broadcasted_iota(jnp.int32, (64, 64), 0)
    col = lax.broadcasted_iota(jnp.int32, (64, 64), 1)
    head = ((row & 15) >> 1) * 8 + (row >> 4) * 2 + (row & 1)
    perm = jnp.where(head == col, 1.0, 0.0).astype(BF16)
    pos = a * 512 + lax.broadcasted_iota(jnp.int32, (64, 512), 1)
    lane = lax.broadcasted_iota(jnp.int32, (64, 128), 1)
    for mb in range(2):
        qp = jnp.dot(perm, q_v[mb], preferred_element_type=F32).astype(BF16)
        scores = jnp.dot(qp, cache_v[mb], preferred_element_type=F32) * SCALE
        visible = pos < len_v[0, mb]
        top = jnp.max(jnp.where(visible, scores, -1e30), axis=1, keepdims=True)
        top = top.astype(BF16).astype(F32)
        weights = jnp.where(visible, jnp.exp(scores - top), 0.0)
        total = jnp.sum(weights, axis=1, keepdims=True)
        acc = lax.dot_general(
            weights.astype(BF16), cache_v[mb, 0:512, :], NT, preferred_element_type=F32
        )
        hi = total.astype(BF16).astype(F32)
        stats = jnp.where(lane == 0, top, jnp.where(lane == 1, hi, total - hi))
        s1_v[:, mb, :, 0:512] = acc.astype(BF16).reshape(4, 16, 512)
        s1_v[:, mb, :, 512:640] = stats.astype(BF16).reshape(4, 16, 128)
    pl.semaphore_wait(barrier, 41)
    for d in FAR4:
        sends.go(s1_v.at[xi(d)], p1_v.at[d - 1], p1_sem.at[d - 1], xdev(d))

    loads[4].wait()
    loads[5].wait()
    for mb in range(2):
        for s in range(2):
            gate = jnp.sum(
                jnp.where(ids_v[mb] == e - c + s, wts_v[mb], 0.0), axis=0, keepdims=True
            )
            gate = jnp.broadcast_to(gate, (128, 128)).T
            for grp in range(4):
                at = grp * 32
                rw_v[s, mb * 64 + grp * 16 : mb * 64 + grp * 16 + 16, :] = jnp.where(
                    first, gate[at : at + 16, :], gate[at + 16 : at + 32, :]
                )

    loads[2].wait()
    for d in FAR4:
        sends.go(wvt_v.at[a], wvt_v.at[a], wsem.at[d - 1], xdev(d))

    for d in range(1, 4):
        arrived(p1_v.at[d - 1], p1_sem.at[d - 1])
    blocks = [s1_v[a]] + [p1_v[d] for d in range(3)]
    blocks = [b.astype(F32).reshape(32, 640) for b in blocks]
    tops = [b[:, 512:513] for b in blocks]
    row_top = jnp.maximum(jnp.maximum(tops[0], tops[1]), jnp.maximum(tops[2], tops[3]))
    ctx_sum = jnp.zeros((32, 512), F32)
    row_total = jnp.zeros((32, 1), F32)
    for b, t in zip(blocks, tops):
        factor = jnp.exp(t - row_top)
        ctx_sum = ctx_sum + b[:, 0:512] * factor
        row_total = row_total + (b[:, 513:514] + b[:, 514:515]) * factor
    context = ctx_sum / row_total
    for mb in range(2):
        for k in range(4):
            c32_v[:, mb * 4 + k, :] = context[
                mb * 16 : (mb + 1) * 16, k * 128 : (k + 1) * 128
            ]
    s2_v[...] = c32_v[...].reshape(8, 16, 128).astype(BF16)

    for s_off in (2, 1, 3, 0):
        for d in FAR4 + (0,):
            for half in (1, 0):
                j = (half + l) % 2 * 4 + (y // 2 + s_off) % 4
                to_e = 4 * j + a
                device = {"attn": xi(d), "exp": to_e}
                if s_off == 0 and d == 0:
                    mine = to_e == e
                    near = pltpu.make_async_copy(s2_v.at[j], p2_v.at[e], big_sem.at[0])
                    when(mine)(near.start)
                    sends.go(
                        s2_v.at[j], p2_v.at[e], big_sem.at[0], device, jnp.logical_not(mine)
                    )
                else:
                    sends.go(s2_v.at[j], p2_v.at[e], big_sem.at[0], device)

    for d in FAR4:
        sends.go(
            wo_hbm.at[:, :, pl.ds(pl.multiple_of(xi(d) * 896, 128), 896)],
            wo_v.at[a],
            wsem.at[2 + d],
            xdev(d),
        )
    loads[6].wait()
    for d in range(1, 4):
        arrived(wvt_v.at[xi(-d)], wsem.at[d - 1])
        arrived(wo_v.at[xi(-d)], wsem.at[2 + d])
    pltpu.make_async_copy(p2_v, p2_v, big_sem.at[0]).wait()
    c2_v[...] = p2_v[...].astype(F32)
    out = jnp.zeros((64, 896), F32)
    for h in range(2):
        rows = [
            jnp.concatenate([c2_v[:, h * 8 + mb * 4 + k, :] for k in range(4)], axis=1)
            for mb in range(2)
        ]
        ctx = jnp.concatenate(rows, axis=0).astype(BF16)
        values = lax.dot_general(
            ctx, wvt_v[:, h].reshape(128, 512), NT, preferred_element_type=F32
        ).astype(BF16)
        out = out + jnp.dot(
            values, wo_v[:, h].reshape(128, 896), preferred_element_type=F32
        )
    for k in range(7):
        s3_v[k] = out[:, k * 128 : (k + 1) * 128].astype(BF16).reshape(4, 16, 128)

    for d in FAR8 + (0,):
        for half in (1, 0):
            for core in (1, 0):
                if d == 0 and half == 0 and core == 0:
                    continue
                to_l, to_c = (l + half) % 2, (c + core) % 2
                src = s3_v.at[jnp.minimum(yi(d), 6), to_l * 2 + to_c]
                device = {"exp": to_l * 16 + yi(d) * 2 + to_c}
                sends.go(src, p3_v.at[e], big_sem.at[1], device, yi(d) < 7)

    halves = [
        (wg_hbm, wgu_v.at[c, :, pl.ds(0, 128)], wgu_v.at[1 - c, :, pl.ds(0, 128)]),
        (wu_hbm, wgu_v.at[c, :, pl.ds(128, 128)], wgu_v.at[1 - c, :, pl.ds(128, 128)]),
        (wd_hbm, wd_v.at[c], wd_v.at[1 - c]),
    ]
    for i, (src, dst, _) in enumerate(halves):
        sends.go(src, dst, core_sem.at[i], core_dev)

    @when(has_tile)
    def _():
        pltpu.make_async_copy(s3_v.at[yc, l * 2 + c], p3_v.at[e], big_sem.at[1]).start()
        loads[3].wait()
        pltpu.make_async_copy(p3_v, p3_v, big_sem.at[1]).wait()
        attended = jnp.sum(p3_v[...].astype(F32), axis=0)
        hidden = res_v[...].astype(F32) + attended
        hid_v[...] = hidden
        ag_v[a, yc, l, g] = (hidden * gain_v[pl.ds(a * 7 + yc, 1), :]).astype(BF16)

    @when(jnp.logical_not(has_tile))
    def _():
        loads[3].wait()

    own = ag_v.at[a, yc, l, g]
    for d in FAR8:
        sends.go(own, own, g_sem.at[d - 1], ydev(d), even, has_tile)
    for d in FAR8:
        sends.go(own, own, g_sem.at[7 + d - 1], zdev(d), odd, first, has_tile)
    for d in FAR4:
        sends.go(own, own, g_sem.at[14 + d - 1], xdev(d), odd, second, has_tile)

    def hidden_copy(i):
        to_e = c * 16 + i
        far = remote(
            f_v.at[i], o_v.at[l, yc], loop_sems.at[i], big_sem.at[2], {"exp": to_e}
        )
        return to_e == e, far

    def hidden_go(i, carry):
        mine, far = hidden_copy(i)

        @when(mine)
        def _():
            pltpu.make_async_copy(f_v.at[i], o_v.at[l, yc], big_sem.at[2]).start()

        pl.when(jnp.logical_not(mine))(far.start)
        return carry

    def hidden_done(i, carry):
        mine, far = hidden_copy(i)
        pl.when(jnp.logical_not(mine))(far.wait_send)
        return carry

    @when(has_tile)
    def _():
        for i in range(16):
            f_v[i] = hid_v[i : i + 1, :]
        lax.fori_loop(0, 16, hidden_go, 0)

    @when(odd & second & has_tile)
    def _():
        for d in NEAR4:
            arrived(ag_v.at[xi(-d), yc, 1, g], g_sem.at[14 + d - 1])

    for d in FAR8:
        blk = ag_v.at[:, yc, 1, g]
        sends.go(blk, blk, g_sem.at[27 + d - 1], ydev(d), odd, second, has_tile)

    @when(even)
    def _():
        for d in NEAR8:

            @when(yi(-d) < 7)
            def _():
                arrived(ag_v.at[a, jnp.minimum(yi(-d), 6), 0, g], g_sem.at[d - 1])

    for d in FAR8:
        blk = ag_v.at[a, :, 0, g]
        sends.go(blk, blk, g_sem.at[17 + d - 1], zdev(d), even)

    @when(first & has_tile)
    def _():
        for d in NEAR8:

            @when(zi(-d) % 2 == 1)
            def _():
                arrived(ag_v.at[a, yc, 1, zi(-d) // 2], g_sem.at[7 + d - 1])

    for d in FAR4:
        blk = ag_v.at[a, yc, 1]
        sends.go(blk, blk, g_sem.at[24 + d - 1], xdev(d), first, has_tile)

    def part(p):
        offset = (0, 2, 6, 4)[p] + l * (1, 5, -3, 1)[p]
        return offset, (z - offset + 8) % 8 // 2

    def pass_on(p):
        offset, from_g = part(p)
        blk = ag_v.at[a, :, 0, from_g]
        if p == 0:

            @when(odd)
            def _():
                arrived(blk, g_sem.at[16 + jnp.maximum(offset, 1)])

        else:
            arrived(blk, g_sem.at[16 + offset])
        for d in FAR4:
            sends.go(blk, blk, g_sem.at[34 + (d - 1) * 4 + p], xdev(d))

    pass_on(0)

    @when(first & has_tile)
    def _():
        for d in NEAR4:
            arrived(ag_v.at[xi(-d), yc, 1], g_sem.at[24 + d - 1])

    blk_y = ag_v.at[:, yc, 1]
    for d in FAR8:
        sends.go(blk_y, blk_y, g_sem.at[46 + d - 1], ydev(d), first, has_tile)

    @when(odd & second)
    def _():
        for d in NEAR8:

            @when(yi(-d) < 7)
            def _():
                arrived(ag_v.at[:, jnp.minimum(yi(-d), 6), 1, g], g_sem.at[27 + d - 1])

    blk_z = ag_v.at[:, :, 1, g]
    for d in FAR8:
        sends.go(blk_z, blk_z, g_sem.at[53 + d - 1], zdev(d), odd, second)

    pass_on(1)
    pass_on(2)
    pass_on(3)

    for p in range(4):
        from_g = part(p)[1]
        for d in NEAR4:
            arrived(ag_v.at[xi(-d), :, 0, from_g], g_sem.at[34 + (d - 1) * 4 + p])
    for d in NEAR8:

        @when(first & (yi(-d) < 7))
        def _():
            arrived(ag_v.at[:, jnp.minimum(yi(-d), 6), 1], g_sem.at[46 + d - 1])

        @when(second & (zi(-d) % 2 == 1))
        def _():
            arrived(ag_v.at[:, :, 1, zi(-d) // 2], g_sem.at[53 + d - 1])

    loads[7].wait()
    loads[8].wait()
    loads[9].wait()
    for i, (_, _, dst) in enumerate(halves):
        arrived(dst, core_sem.at[i])
    pieces = [ag_v[i // 7, i % 7].reshape(128, 128) for i in range(28)]
    square = jnp.zeros((128, 128), F32)
    for i in range(28):
        item = pieces[i].astype(F32) / gain_v[i : i + 1, :]
        square = square + item * item
    inverse = lax.rsqrt(jnp.sum(square, axis=1, keepdims=True) * (1.0 / 3584) + 1e-6)
    rows = jnp.concatenate(pieces, axis=1)
    acts = []
    for s in range(2):
        both = jnp.dot(rows, wgu_v[s], preferred_element_type=F32) * inverse
        gate = both[:, 0:128]
        acts.append(gate / (1.0 + jnp.exp(-gate)) * both[:, 128:256] * rw_v[s])
    act = jnp.concatenate(acts, axis=1).astype(BF16)
    def target(p):
        offset = (4, 2, 6, 0)[p] + (l + c) % 2 * (-1, 3, -5, 7)[p]
        return offset, (z + offset) % 8 // 2

    for n, d in enumerate(QUARTERS):
        x = xi(d)
        down = jnp.dot(
            act,
            wd_v[:, :, pl.ds(pl.multiple_of(x * 896, 128), 896)].reshape(256, 896),
            preferred_element_type=F32,
        )
        for mb in range(2):
            for k in range(7):
                unit_v[n % 2, :, mb * 7 + k, :] = down[
                    mb * 64 : (mb + 1) * 64, k * 128 : (k + 1) * 128
                ]
        qs_v[x] = unit_v[n % 2].astype(BF16).reshape(4, 8, 2, 16, 128)
        if d > 0:
            for p in range(4):
                sends.go(
                    qs_v.at[x, target(p)[1], :, 0],
                    r1x_v.at[d - 1, p],
                    r_sem.at[(d - 1) * 4 + p],
                    xdev(d),
                )
        for to in FAR8:
            sends.go(
                qs_v.at[x, :, yi(to), 1],
                r1y_v.at[to - 1, n],
                r_sem.at[12 + (to - 1) * 4 + n],
                ydev(to),
                first,
            )
            sends.go(
                qs_v.at[x, zi(to) // 2, :, 1],
                r1z_v.at[to - 1, n],
                r_sem.at[40 + (to - 1) * 4 + n],
                zdev(to),
                second,
                zi(to) % 2 == 1,
            )

    def total_of(blocks):
        result = blocks[0].astype(F32)
        for blk in blocks[1:]:
            result = result + blk.astype(F32)
        return result

    def take(ref, base, items):
        for i in items:
            arrived(ref.at[i], r_sem.at[base + i])
        return [ref[i] for i in items]

    for p in range(4):
        offset, to_g = target(p)
        result = qs_v[a, to_g, :, 0].astype(F32)
        for d in NEAR4:
            arrived(r1x_v.at[d - 1, p], r_sem.at[(d - 1) * 4 + p])
            result = result + r1x_v[d - 1, p].astype(F32)
        s1x_v[p] = result.astype(BF16)
        device = {"grp": to_g, "exp": c * 16 + y * 2 + c}
        slot = jnp.maximum(offset - 1, 0)
        conds = (l != c,) if p == 3 else ()
        sends.go(s1x_v.at[p], r2x_v.at[slot], r_sem.at[68 + slot], device, *conds)

        n, d = p, QUARTERS[p]

        @when(first)
        def _():
            blocks = [qs_v[xi(d), :, y, 1]]
            for i in range(7):
                arrived(r1y_v.at[i, n], r_sem.at[12 + i * 4 + n])
                blocks.append(r1y_v[i, n])
            s1y_v[n] = total_of(blocks).astype(BF16)

        if d > 0:
            sends.go(s1y_v.at[n], r2y_v.at[d - 1], r_sem.at[75 + d - 1], xdev(d), first)

    @when(second & odd)
    def _():
        for n, d in enumerate(QUARTERS):
            blocks = [qs_v[xi(d), g, :, 1]]
            for i in range(7):
                arrived(r1z_v.at[i, n], r_sem.at[40 + i * 4 + n])
                blocks.append(r1z_v[i, n])
            s1z_v[xi(d)] = total_of(blocks).astype(BF16)

    for d in FAR8:
        sends.go(
            s1z_v.at[:, yi(d)], r2z_v.at[d - 1], r_sem.at[78 + d - 1], ydev(d), second, odd
        )

    @when(first)
    def _():
        s2y_v[...] = total_of([s1y_v[3]] + take(r2y_v, 75, range(3))).astype(BF16)

    for d in FAR8 + (0,):
        device = {"grp": zi(d) // 2, "exp": y * 2 + 1}
        sends.go(
            s2y_v.at[zi(d) // 2], r3_v.at[d], r_sem.at[85 + d], device, first, zi(d) % 2 == 0
        )

    @when(l == c)
    def _():
        s2x_v[...] = total_of([s1x_v[3]] + take(r2x_v, 68, range(7))).astype(BF16)

    for d in FAR8 + (0,):
        device = {"exp": l * 16 + yi(d) * 2}
        conds = (l == c, second) if d == 0 else (l == c,)
        sends.go(s2x_v.at[yi(d)], r3_v.at[d], r_sem.at[85 + d], device, *conds)

    @when(second & odd)
    def _():
        s2z_v[...] = total_of([s1z_v[:, y]] + take(r2z_v, 78, range(7))).astype(BF16)

    for d in FAR4:
        sends.go(s2z_v.at[xi(d)], r3_v.at[d], r_sem.at[85 + d], xdev(d), second, odd)

    pltpu.make_async_copy(o_v, o_v, big_sem.at[2]).wait()
    sends.drain()

    @when(has_tile)
    def _():
        lax.fori_loop(0, 16, hidden_done, 0)

    @when(even & first)
    def _():
        fin_v[...] = total_of([s2x_v[y]] + take(r3_v, 85, range(1, 8)))

    @when(l != c)
    def _():
        fin_v[...] = total_of(take(r3_v, 85, range(8)))

    @when(odd & second)
    def _():
        fin_v[...] = total_of([s2z_v[a]] + take(r3_v, 85, range(1, 4)))

    rows = [
        jnp.concatenate(
            [fin_v[mb * 7 + k : mb * 7 + k + 1, :] + o_v[mb, k] for k in range(7)], axis=1
        )
        for mb in range(2)
    ]
    out_ref[...] = jnp.concatenate(rows, axis=0).astype(BF16)


def body(
    resid,
    queries,
    cache,
    lengths,
    w_value,
    w_out,
    norm_gain,
    route_ids,
    route_weights,
    w_gate,
    w_up,
    w_down,
):
    hbm = pl.BlockSpec(memory_space=pl.ANY)
    vmem = pl.BlockSpec(memory_space=pltpu.VMEM)

    def bf(*shape):
        return pltpu.VMEM(shape, BF16)

    def f32(*shape):
        return pltpu.VMEM(shape, F32)

    def dma(count):
        return pltpu.SemaphoreType.DMA((count,))

    return pl.pallas_call(
        kernel,
        out_shape=jax.ShapeDtypeStruct((2, 896), BF16),
        in_specs=[hbm] * 12,
        out_specs=vmem,
        scratch_shapes=[
            pltpu.SMEM((1, 2), jnp.int32),
            bf(28, 128),
            bf(2, 64, 576),
            bf(2, 576, 512),
            bf(16, 128),
            pltpu.VMEM((2, 8, 128), jnp.int32),
            f32(2, 8, 128),
            bf(4, 2, 32, 512),
            bf(4, 2, 32, 896),
            bf(2, 3584, 256),
            bf(2, 128, 3584),
            f32(2, 128, 128),
            f32(28, 128),
            bf(4, 2, 16, 640),
            bf(3, 2, 16, 640),
            f32(16, 8, 128),
            bf(8, 16, 128),
            bf(32, 16, 128),
            f32(32, 16, 128),
            bf(7, 4, 16, 128),
            bf(32, 16, 128),
            f32(16, 128),
            bf(4, 7, 2, 4, 16, 128),
            bf(4, 4, 8, 2, 16, 128),
            bf(3, 4, 8, 16, 128),
            bf(7, 4, 4, 16, 128),
            bf(7, 4, 8, 16, 128),
            bf(4, 8, 16, 128),
            bf(4, 4, 16, 128),
            bf(4, 8, 16, 128),
            bf(7, 8, 16, 128),
            bf(3, 4, 16, 128),
            bf(7, 4, 16, 128),
            bf(8, 16, 128),
            bf(4, 16, 128),
            bf(4, 16, 128),
            bf(8, 16, 128),
            f32(16, 1, 128),
            f32(2, 7, 1, 128),
            f32(2, 64, 16, 128),
            f32(16, 128),
            dma(12),
            dma(SEND_SEMS),
            dma(16),
            dma(6),
            dma(3),
            dma(3),
            dma(60),
            dma(3),
            dma(93),
        ],
        compiler_params=pltpu.CompilerParams(
            collective_id=0, has_side_effects=True, vmem_limit_bytes=56 * 1024 * 1024
        ),
        name="layer",
    )(
        lengths.reshape(1, 2),
        norm_gain.reshape(28, 128),
        queries[:, 0],
        jnp.swapaxes(cache[:, 0], 1, 2),
        resid,
        jnp.swapaxes(route_ids, 1, 2),
        jnp.swapaxes(route_weights, 1, 2),
        jnp.swapaxes(w_value, 1, 2),
        w_out,
        w_gate[0],
        w_up[0],
        w_down[0],
    ).reshape(2, 1, 896)


def solution(mesh):
    return jax.shard_map(
        body,
        mesh=mesh,
        in_specs=(
            P(None, "grp", None),
            P(None, ("grp", "exp"), None, None),
            P(None, ("grp", "exp"), "attn", None),
            P(None, ("grp", "exp")),
            P("exp", None, "attn"),
            P("exp", "attn", None),
            P(),
            P(),
            P(),
            P("exp", None, ("attn", "grp")),
            P("exp", None, ("attn", "grp")),
            P("exp", ("attn", "grp"), None),
        ),
        out_specs=P(None, ("grp", "exp"), "attn"),
        check_vma=False,
    )
```

```python
import jax
import jax.numpy as jnp
from jax import lax
from jax.experimental import pallas as pl
from jax.experimental.pallas import tpu as pltpu
from jax.sharding import PartitionSpec as P

MESH = pl.DeviceIdType.MESH
F32 = jnp.float32
BF16 = jnp.bfloat16
SCALE = (128 + 64) ** -0.5
NT = (((1,), (1,)), ((), ()))


def remote(src, dst, send_sem, recv_sem, device):
    return pltpu.make_async_remote_copy(
        src_ref=src,
        dst_ref=dst,
        send_sem=send_sem,
        recv_sem=recv_sem,
        device_id=device,
        device_id_type=MESH,
    )


class Sends:
    def __init__(self, sems):
        self.sems = sems
        self.used = 0
        self.pending = []

    def go(self, src, dst, recv_sem, device, *conds):
        copy = remote(src, dst, self.sems.at[self.used], recv_sem, device)
        self.used += 1
        cond = None
        for item in conds:
            cond = item if cond is None else cond & item
        if cond is None:
            copy.start()
        else:
            pl.when(cond)(copy.start)
        self.pending.append((cond, copy))

    def drain(self, count=None):
        count = len(self.pending) if count is None else count
        for cond, copy in self.pending[:count]:
            if cond is None:
                copy.wait_send()
            else:
                pl.when(cond)(copy.wait_send)
        self.pending = self.pending[count:]


FAR8 = (4, 3, 5, 2, 6, 1, 7)
FAR4 = (2, 1, 3)
QUARTERS = (2, 1, 3, 0)
NEAR8 = (1, 7, 2, 6, 3, 5, 4)
NEAR4 = (1, 3, 2)
SEND_SEMS = 290


def kernel(
    len_hbm,
    gain_hbm,
    q_hbm,
    cache_hbm,
    resid_hbm,
    ids_hbm,
    wts_hbm,
    wv_hbm,
    wo_hbm,
    wg_hbm,
    wu_hbm,
    wd_hbm,
    out_ref,
    len_v,
    gain16_v,
    q_v,
    cache_v,
    res_v,
    ids_v,
    wts_v,
    wvt_v,
    wo_v,
    wgu_v,
    wd_v,
    rw_v,
    gain_v,
    s1_v,
    p1_v,
    c32_v,
    s2_v,
    p2_v,
    c2_v,
    s3_v,
    p3_v,
    hid_v,
    ag_v,
    qs_v,
    r1x_v,
    r1y_v,
    r1z_v,
    s1x_v,
    s1y_v,
    s1z_v,
    r2x_v,
    r2y_v,
    r2z_v,
    s2x_v,
    s2y_v,
    s2z_v,
    r3_v,
    f_v,
    o_v,
    unit_v,
    fin_v,
    lsem,
    send_sems,
    loop_sems,
    wsem,
    p1_sem,
    big_sem,
    g_sem,
    core_sem,
    r_sem,
):
    a = lax.axis_index("attn")
    g = lax.axis_index("grp")
    e = lax.axis_index("exp")
    c = e % 2
    y = (e // 2) % 8
    l = e // 16
    z = 2 * g + l
    yc = jnp.minimum(y, 6)
    has_tile = y < 7
    even = l == 0
    odd = l == 1
    first = c == 0
    second = c == 1
    sends = Sends(send_sems)
    when = pl.when

    def xi(d):
        return (a + d + 4) % 4

    def yi(d):
        return (y + d + 8) % 8

    def zi(d):
        return (z + d + 8) % 8

    def xdev(d):
        return {"attn": xi(d)}

    def ydev(d):
        return {"exp": l * 16 + yi(d) * 2 + c}

    def zdev(d):
        return {"grp": zi(d) // 2, "exp": (zi(d) % 2) * 16 + y * 2 + c}

    core_dev = {"exp": e + 1 - 2 * c}

    def arrived(dst, sem):
        remote(dst, dst, send_sems.at[0], sem, core_dev).wait_recv()

    chunk = pl.multiple_of((a * 7 + yc) * 128, 128)
    loads = [
        pltpu.make_async_copy(src, dst, lsem.at[i])
        for i, (src, dst) in enumerate(
            [
                (q_hbm, q_v),
                (cache_hbm, cache_v),
                (wv_hbm, wvt_v.at[a]),
                (
                    resid_hbm.at[l, pl.ds(pl.multiple_of(c * 16, 16), 16), pl.ds(chunk, 128)],
                    res_v,
                ),
                (ids_hbm, ids_v),
                (wts_hbm, wts_v),
                (
                    wo_hbm.at[:, :, pl.ds(pl.multiple_of(a * 896, 128), 896)],
                    wo_v.at[a],
                ),
                (wg_hbm, wgu_v.at[c, :, pl.ds(0, 128)]),
                (wu_hbm, wgu_v.at[c, :, pl.ds(128, 128)]),
                (wd_hbm, wd_v.at[c]),
                (len_hbm, len_v),
                (gain_hbm, gain16_v),
            ]
        )
    ]
    for i in (1, 0, 10):
        loads[i].start()

    barrier = pltpu.get_barrier_semaphore()

    def greet(device):
        pl.semaphore_signal(barrier, inc=1, device_id=device, device_id_type=MESH)


    def greet_plane(i, carry):
        greet({"exp": (e + i) % 32})
        return carry

    lax.fori_loop(8, 32, greet_plane, 0)
    for d in FAR8:
        greet(zdev(d))
    for d in FAR4:
        greet(xdev(d))
    lax.fori_loop(1, 8, greet_plane, 0)

    for i in (11, 2, 3, 4, 5, 6, 7, 8, 9):
        loads[i].start()
    loads[11].wait()
    gain_v[...] = gain16_v[...].astype(F32)
    unit_v[:, :, 8:16, :] = jnp.zeros((2, 64, 8, 128), F32)

    loads[10].wait()
    loads[0].wait()
    loads[1].wait()
    row = lax.broadcasted_iota(jnp.int32, (64, 64), 0)
    col = lax.broadcasted_iota(jnp.int32, (64, 64), 1)
    head = ((row & 15) >> 1) * 8 + (row >> 4) * 2 + (row & 1)
    perm = jnp.where(head == col, 1.0, 0.0).astype(BF16)
    pos = a * 512 + lax.broadcasted_iota(jnp.int32, (64, 512), 1)
    lane = lax.broadcasted_iota(jnp.int32, (64, 128), 1)
    for mb in range(2):
        qp = jnp.dot(perm, q_v[mb], preferred_element_type=F32).astype(BF16)
        scores = jnp.dot(qp, cache_v[mb], preferred_element_type=F32) * SCALE
        visible = pos < len_v[0, mb]
        top = jnp.max(jnp.where(visible, scores, -1e30), axis=1, keepdims=True)
        top = top.astype(BF16).astype(F32)
        weights = jnp.where(visible, jnp.exp(scores - top), 0.0)
        total = jnp.sum(weights, axis=1, keepdims=True)
        acc = lax.dot_general(
            weights.astype(BF16), cache_v[mb, 0:512, :], NT, preferred_element_type=F32
        )
        hi = total.astype(BF16).astype(F32)
        stats = jnp.where(lane == 0, top, jnp.where(lane == 1, hi, total - hi))
        s1_v[:, mb, :, 0:512] = acc.astype(BF16).reshape(4, 16, 512)
        s1_v[:, mb, :, 512:640] = stats.astype(BF16).reshape(4, 16, 128)
    pl.semaphore_wait(barrier, 41)
    for d in FAR4:
        sends.go(s1_v.at[xi(d)], p1_v.at[d - 1], p1_sem.at[d - 1], xdev(d))

    loads[4].wait()
    loads[5].wait()
    for mb in range(2):
        for s in range(2):
            gate = jnp.sum(
                jnp.where(ids_v[mb] == e - c + s, wts_v[mb], 0.0), axis=0, keepdims=True
            )
            gate = jnp.broadcast_to(gate, (128, 128)).T
            for grp in range(4):
                at = grp * 32
                rw_v[s, mb * 64 + grp * 16 : mb * 64 + grp * 16 + 16, :] = jnp.where(
                    first, gate[at : at + 16, :], gate[at + 16 : at + 32, :]
                )

    loads[2].wait()
    for d in FAR4:
        sends.go(wvt_v.at[a], wvt_v.at[a], wsem.at[d - 1], xdev(d))

    for d in range(1, 4):
        arrived(p1_v.at[d - 1], p1_sem.at[d - 1])
    blocks = [s1_v[a]] + [p1_v[d] for d in range(3)]
    blocks = [b.astype(F32).reshape(32, 640) for b in blocks]
    tops = [b[:, 512:513] for b in blocks]
    row_top = jnp.maximum(jnp.maximum(tops[0], tops[1]), jnp.maximum(tops[2], tops[3]))
    ctx_sum = jnp.zeros((32, 512), F32)
    row_total = jnp.zeros((32, 1), F32)
    for b, t in zip(blocks, tops):
        factor = jnp.exp(t - row_top)
        ctx_sum = ctx_sum + b[:, 0:512] * factor
        row_total = row_total + (b[:, 513:514] + b[:, 514:515]) * factor
    context = ctx_sum / row_total
    for mb in range(2):
        for k in range(4):
            c32_v[:, mb * 4 + k, :] = context[
                mb * 16 : (mb + 1) * 16, k * 128 : (k + 1) * 128
            ]
    s2_v[...] = c32_v[...].reshape(8, 16, 128).astype(BF16)

    for s_off in (2, 1, 3, 0):
        for d in FAR4 + (0,):
            for half in (1, 0):
                j = (half + l) % 2 * 4 + (y // 2 + s_off) % 4
                to_e = 4 * j + a
                device = {"attn": xi(d), "exp": to_e}
                if s_off == 0 and d == 0:
                    mine = to_e == e
                    near = pltpu.make_async_copy(s2_v.at[j], p2_v.at[e], big_sem.at[0])
                    when(mine)(near.start)
                    sends.go(
                        s2_v.at[j], p2_v.at[e], big_sem.at[0], device, jnp.logical_not(mine)
                    )
                else:
                    sends.go(s2_v.at[j], p2_v.at[e], big_sem.at[0], device)

    for d in FAR4:
        sends.go(
            wo_hbm.at[:, :, pl.ds(pl.multiple_of(xi(d) * 896, 128), 896)],
            wo_v.at[a],
            wsem.at[2 + d],
            xdev(d),
        )
    loads[6].wait()
    for d in range(1, 4):
        arrived(wvt_v.at[xi(-d)], wsem.at[d - 1])
        arrived(wo_v.at[xi(-d)], wsem.at[2 + d])
    pltpu.make_async_copy(p2_v, p2_v, big_sem.at[0]).wait()
    c2_v[...] = p2_v[...].astype(F32)
    out = jnp.zeros((64, 896), F32)
    for h in range(2):
        rows = [
            jnp.concatenate([c2_v[:, h * 8 + mb * 4 + k, :] for k in range(4)], axis=1)
            for mb in range(2)
        ]
        ctx = jnp.concatenate(rows, axis=0).astype(BF16)
        values = lax.dot_general(
            ctx, wvt_v[:, h].reshape(128, 512), NT, preferred_element_type=F32
        ).astype(BF16)
        out = out + jnp.dot(
            values, wo_v[:, h].reshape(128, 896), preferred_element_type=F32
        )
    for k in range(7):
        s3_v[k] = out[:, k * 128 : (k + 1) * 128].astype(BF16).reshape(4, 16, 128)

    for d in FAR8 + (0,):
        for half in (1, 0):
            for core in (1, 0):
                if d == 0 and half == 0 and core == 0:
                    continue
                to_l, to_c = (l + half) % 2, (c + core) % 2
                src = s3_v.at[jnp.minimum(yi(d), 6), to_l * 2 + to_c]
                device = {"exp": to_l * 16 + yi(d) * 2 + to_c}
                sends.go(src, p3_v.at[e], big_sem.at[1], device, yi(d) < 7)

    halves = [
        (wg_hbm, wgu_v.at[c, :, pl.ds(0, 128)], wgu_v.at[1 - c, :, pl.ds(0, 128)]),
        (wu_hbm, wgu_v.at[c, :, pl.ds(128, 128)], wgu_v.at[1 - c, :, pl.ds(128, 128)]),
        (wd_hbm, wd_v.at[c], wd_v.at[1 - c]),
    ]
    for i, (src, dst, _) in enumerate(halves):
        sends.go(src, dst, core_sem.at[i], core_dev)

    @when(has_tile)
    def _():
        pltpu.make_async_copy(s3_v.at[yc, l * 2 + c], p3_v.at[e], big_sem.at[1]).start()
        loads[3].wait()
        pltpu.make_async_copy(p3_v, p3_v, big_sem.at[1]).wait()
        attended = jnp.sum(p3_v[...].astype(F32), axis=0)
        hidden = res_v[...].astype(F32) + attended
        hid_v[...] = hidden
        ag_v[a, yc, l, g] = (hidden * gain_v[pl.ds(a * 7 + yc, 1), :]).astype(BF16)

    @when(jnp.logical_not(has_tile))
    def _():
        loads[3].wait()

    own = ag_v.at[a, yc, l, g]
    for d in FAR8:
        sends.go(own, own, g_sem.at[d - 1], ydev(d), even, has_tile)
    for d in FAR8:
        sends.go(own, own, g_sem.at[7 + d - 1], zdev(d), odd, first, has_tile)
    for d in FAR4:
        sends.go(own, own, g_sem.at[14 + d - 1], xdev(d), odd, second, has_tile)

    def hidden_copy(i):
        to_e = c * 16 + i
        far = remote(
            f_v.at[i], o_v.at[l, yc], loop_sems.at[i], big_sem.at[2], {"exp": to_e}
        )
        return to_e == e, far

    def hidden_go(i, carry):
        mine, far = hidden_copy(i)

        @when(mine)
        def _():
            pltpu.make_async_copy(f_v.at[i], o_v.at[l, yc], big_sem.at[2]).start()

        pl.when(jnp.logical_not(mine))(far.start)
        return carry

    def hidden_done(i, carry):
        mine, far = hidden_copy(i)
        pl.when(jnp.logical_not(mine))(far.wait_send)
        return carry

    @when(odd & second & has_tile)
    def _():
        for d in NEAR4:
            arrived(ag_v.at[xi(-d), yc, 1, g], g_sem.at[14 + d - 1])

    for d in FAR8:
        blk = ag_v.at[:, yc, 1, g]
        sends.go(blk, blk, g_sem.at[27 + d - 1], ydev(d), odd, second, has_tile)

    @when(even)
    def _():
        for d in NEAR8:

            @when(yi(-d) < 7)
            def _():
                arrived(ag_v.at[a, jnp.minimum(yi(-d), 6), 0, g], g_sem.at[d - 1])

    for d in FAR8:
        blk = ag_v.at[a, :, 0, g]
        sends.go(blk, blk, g_sem.at[17 + d - 1], zdev(d), even)

    @when(first & has_tile)
    def _():
        for d in NEAR8:

            @when(zi(-d) % 2 == 1)
            def _():
                arrived(ag_v.at[a, yc, 1, zi(-d) // 2], g_sem.at[7 + d - 1])

    for d in FAR4:
        blk = ag_v.at[a, yc, 1]
        sends.go(blk, blk, g_sem.at[24 + d - 1], xdev(d), first, has_tile)

    def part(p):
        offset = (0, 2, 6, 4)[p] + l * (1, 5, -3, 1)[p]
        return offset, (z - offset + 8) % 8 // 2

    def pass_on(p):
        offset, from_g = part(p)
        blk = ag_v.at[a, :, 0, from_g]
        if p == 0:

            @when(odd)
            def _():
                arrived(blk, g_sem.at[16 + jnp.maximum(offset, 1)])

        else:
            arrived(blk, g_sem.at[16 + offset])
        for d in FAR4:
            sends.go(blk, blk, g_sem.at[34 + (d - 1) * 4 + p], xdev(d))

    before = len(sends.pending)
    pass_on(0)

    @when(first & has_tile)
    def _():
        for d in NEAR4:
            arrived(ag_v.at[xi(-d), yc, 1], g_sem.at[24 + d - 1])

    blk_y = ag_v.at[:, yc, 1]
    for d in FAR8:
        sends.go(blk_y, blk_y, g_sem.at[46 + d - 1], ydev(d), first, has_tile)

    @when(odd & second)
    def _():
        for d in NEAR8:

            @when(yi(-d) < 7)
            def _():
                arrived(ag_v.at[:, jnp.minimum(yi(-d), 6), 1, g], g_sem.at[27 + d - 1])

    blk_z = ag_v.at[:, :, 1, g]
    for d in FAR8:
        sends.go(blk_z, blk_z, g_sem.at[53 + d - 1], zdev(d), odd, second)

    pass_on(1)
    pass_on(2)
    pass_on(3)
    @when(has_tile)
    def _():
        for i in range(16):
            f_v[i] = hid_v[i : i + 1, :]
        lax.fori_loop(0, 16, hidden_go, 0)

    sends.drain(before)

    for p in range(4):
        from_g = part(p)[1]
        for d in NEAR4:
            arrived(ag_v.at[xi(-d), :, 0, from_g], g_sem.at[34 + (d - 1) * 4 + p])
    for d in NEAR8:

        @when(first & (yi(-d) < 7))
        def _():
            arrived(ag_v.at[:, jnp.minimum(yi(-d), 6), 1], g_sem.at[46 + d - 1])

        @when(second & (zi(-d) % 2 == 1))
        def _():
            arrived(ag_v.at[:, :, 1, zi(-d) // 2], g_sem.at[53 + d - 1])

    loads[7].wait()
    loads[8].wait()
    loads[9].wait()
    for i, (_, _, dst) in enumerate(halves):
        arrived(dst, core_sem.at[i])
    pieces = [ag_v[i // 7, i % 7].reshape(128, 128) for i in range(28)]
    square = jnp.zeros((128, 128), F32)
    for i in range(28):
        item = pieces[i].astype(F32) / gain_v[i : i + 1, :]
        square = square + item * item
    inverse = lax.rsqrt(jnp.sum(square, axis=1, keepdims=True) * (1.0 / 3584) + 1e-6)
    rows = jnp.concatenate(pieces, axis=1)
    acts = []
    for s in range(2):
        both = jnp.dot(rows, wgu_v[s], preferred_element_type=F32) * inverse
        gate = both[:, 0:128]
        acts.append(gate / (1.0 + jnp.exp(-gate)) * both[:, 128:256] * rw_v[s])
    act = jnp.concatenate(acts, axis=1).astype(BF16)
    def target(p):
        offset = (4, 2, 6, 0)[p] + (l + c) % 2 * (-1, 3, -5, 7)[p]
        return offset, (z + offset) % 8 // 2

    before = len(sends.pending)
    for n, d in enumerate(QUARTERS):
        x = xi(d)
        down = jnp.dot(
            act,
            wd_v[:, :, pl.ds(pl.multiple_of(x * 896, 128), 896)].reshape(256, 896),
            preferred_element_type=F32,
        )
        for mb in range(2):
            for k in range(7):
                unit_v[n % 2, :, mb * 7 + k, :] = down[
                    mb * 64 : (mb + 1) * 64, k * 128 : (k + 1) * 128
                ]
        qs_v[x] = unit_v[n % 2].astype(BF16).reshape(4, 8, 2, 16, 128)
        if d > 0:
            for p in range(4):
                sends.go(
                    qs_v.at[x, target(p)[1], :, 0],
                    r1x_v.at[d - 1, p],
                    r_sem.at[(d - 1) * 4 + p],
                    xdev(d),
                )
        for to in FAR8:
            sends.go(
                qs_v.at[x, :, yi(to), 1],
                r1y_v.at[to - 1, n],
                r_sem.at[12 + (to - 1) * 4 + n],
                ydev(to),
                first,
            )
            sends.go(
                qs_v.at[x, zi(to) // 2, :, 1],
                r1z_v.at[to - 1, n],
                r_sem.at[40 + (to - 1) * 4 + n],
                zdev(to),
                second,
                zi(to) % 2 == 1,
            )

    sends.drain(before)
    before = len(sends.pending)

    def total_of(blocks):
        result = blocks[0].astype(F32)
        for blk in blocks[1:]:
            result = result + blk.astype(F32)
        return result

    def take(ref, base, items):
        for i in items:
            arrived(ref.at[i], r_sem.at[base + i])
        return [ref[i] for i in items]

    for p in range(4):
        offset, to_g = target(p)
        result = qs_v[a, to_g, :, 0].astype(F32)
        for d in NEAR4:
            arrived(r1x_v.at[d - 1, p], r_sem.at[(d - 1) * 4 + p])
            result = result + r1x_v[d - 1, p].astype(F32)
        s1x_v[p] = result.astype(BF16)
        device = {"grp": to_g, "exp": c * 16 + y * 2 + c}
        slot = jnp.maximum(offset - 1, 0)
        conds = (l != c,) if p == 3 else ()
        sends.go(s1x_v.at[p], r2x_v.at[slot], r_sem.at[68 + slot], device, *conds)

    for n, d in enumerate(QUARTERS):

        @when(first)
        def _():
            blocks = [qs_v[xi(d), :, y, 1]]
            for i in range(7):
                arrived(r1y_v.at[i, n], r_sem.at[12 + i * 4 + n])
                blocks.append(r1y_v[i, n])
            s1y_v[n] = total_of(blocks).astype(BF16)

        if d > 0:
            sends.go(s1y_v.at[n], r2y_v.at[d - 1], r_sem.at[75 + d - 1], xdev(d), first)

    @when(second & odd)
    def _():
        for n, d in enumerate(QUARTERS):
            blocks = [qs_v[xi(d), g, :, 1]]
            for i in range(7):
                arrived(r1z_v.at[i, n], r_sem.at[40 + i * 4 + n])
                blocks.append(r1z_v[i, n])
            s1z_v[xi(d)] = total_of(blocks).astype(BF16)

    for d in FAR8:
        sends.go(
            s1z_v.at[:, yi(d)], r2z_v.at[d - 1], r_sem.at[78 + d - 1], ydev(d), second, odd
        )
    sends.drain(before)

    @when(first)
    def _():
        s2y_v[...] = total_of([s1y_v[3]] + take(r2y_v, 75, range(3))).astype(BF16)

    for d in FAR8 + (0,):
        device = {"grp": zi(d) // 2, "exp": y * 2 + 1}
        sends.go(
            s2y_v.at[zi(d) // 2], r3_v.at[d], r_sem.at[85 + d], device, first, zi(d) % 2 == 0
        )

    @when(l == c)
    def _():
        s2x_v[...] = total_of([s1x_v[3]] + take(r2x_v, 68, range(7))).astype(BF16)

    for d in FAR8 + (0,):
        device = {"exp": l * 16 + yi(d) * 2}
        conds = (l == c, second) if d == 0 else (l == c,)
        sends.go(s2x_v.at[yi(d)], r3_v.at[d], r_sem.at[85 + d], device, *conds)

    @when(second & odd)
    def _():
        s2z_v[...] = total_of([s1z_v[:, y]] + take(r2z_v, 78, range(7))).astype(BF16)

    for d in FAR4:
        sends.go(s2z_v.at[xi(d)], r3_v.at[d], r_sem.at[85 + d], xdev(d), second, odd)

    pltpu.make_async_copy(o_v, o_v, big_sem.at[2]).wait()
    sends.drain()

    @when(has_tile)
    def _():
        lax.fori_loop(0, 16, hidden_done, 0)

    @when(even & first)
    def _():
        fin_v[...] = total_of([s2x_v[y]] + take(r3_v, 85, range(1, 8)))

    @when(l != c)
    def _():
        fin_v[...] = total_of(take(r3_v, 85, range(8)))

    @when(odd & second)
    def _():
        fin_v[...] = total_of([s2z_v[a]] + take(r3_v, 85, range(1, 4)))

    rows = [
        jnp.concatenate(
            [fin_v[mb * 7 + k : mb * 7 + k + 1, :] + o_v[mb, k] for k in range(7)], axis=1
        )
        for mb in range(2)
    ]
    out_ref[...] = jnp.concatenate(rows, axis=0).astype(BF16)


def body(
    resid,
    queries,
    cache,
    lengths,
    w_value,
    w_out,
    norm_gain,
    route_ids,
    route_weights,
    w_gate,
    w_up,
    w_down,
):
    hbm = pl.BlockSpec(memory_space=pl.ANY)
    vmem = pl.BlockSpec(memory_space=pltpu.VMEM)

    def bf(*shape):
        return pltpu.VMEM(shape, BF16)

    def f32(*shape):
        return pltpu.VMEM(shape, F32)

    def dma(count):
        return pltpu.SemaphoreType.DMA((count,))

    return pl.pallas_call(
        kernel,
        out_shape=jax.ShapeDtypeStruct((2, 896), BF16),
        in_specs=[hbm] * 12,
        out_specs=vmem,
        scratch_shapes=[
            pltpu.SMEM((1, 2), jnp.int32),
            bf(28, 128),
            bf(2, 64, 576),
            bf(2, 576, 512),
            bf(16, 128),
            pltpu.VMEM((2, 8, 128), jnp.int32),
            f32(2, 8, 128),
            bf(4, 2, 32, 512),
            bf(4, 2, 32, 896),
            bf(2, 3584, 256),
            bf(2, 128, 3584),
            f32(2, 128, 128),
            f32(28, 128),
            bf(4, 2, 16, 640),
            bf(3, 2, 16, 640),
            f32(16, 8, 128),
            bf(8, 16, 128),
            bf(32, 16, 128),
            f32(32, 16, 128),
            bf(7, 4, 16, 128),
            bf(32, 16, 128),
            f32(16, 128),
            bf(4, 7, 2, 4, 16, 128),
            bf(4, 4, 8, 2, 16, 128),
            bf(3, 4, 8, 16, 128),
            bf(7, 4, 4, 16, 128),
            bf(7, 4, 8, 16, 128),
            bf(4, 8, 16, 128),
            bf(4, 4, 16, 128),
            bf(4, 8, 16, 128),
            bf(7, 8, 16, 128),
            bf(3, 4, 16, 128),
            bf(7, 4, 16, 128),
            bf(8, 16, 128),
            bf(4, 16, 128),
            bf(4, 16, 128),
            bf(8, 16, 128),
            f32(16, 1, 128),
            f32(2, 7, 1, 128),
            f32(2, 64, 16, 128),
            f32(16, 128),
            dma(12),
            dma(SEND_SEMS),
            dma(16),
            dma(6),
            dma(3),
            dma(3),
            dma(60),
            dma(3),
            dma(93),
        ],
        compiler_params=pltpu.CompilerParams(
            collective_id=0, has_side_effects=True, vmem_limit_bytes=56 * 1024 * 1024
        ),
        name="layer",
    )(
        lengths.reshape(1, 2),
        norm_gain.reshape(28, 128),
        queries[:, 0],
        jnp.swapaxes(cache[:, 0], 1, 2),
        resid,
        jnp.swapaxes(route_ids, 1, 2),
        jnp.swapaxes(route_weights, 1, 2),
        jnp.swapaxes(w_value, 1, 2),
        w_out,
        w_gate[0],
        w_up[0],
        w_down[0],
    ).reshape(2, 1, 896)


def solution(mesh):
    return jax.shard_map(
        body,
        mesh=mesh,
        in_specs=(
            P(None, "grp", None),
            P(None, ("grp", "exp"), None, None),
            P(None, ("grp", "exp"), "attn", None),
            P(None, ("grp", "exp")),
            P("exp", None, "attn"),
            P("exp", "attn", None),
            P(),
            P(),
            P(),
            P("exp", None, ("attn", "grp")),
            P("exp", None, ("attn", "grp")),
            P("exp", ("attn", "grp"), None),
        ),
        out_specs=P(None, ("grp", "exp"), "attn"),
        check_vma=False,
    )
```
